128 devices in a mesh: seq: 8 (over y_hi, x), tensor: 16 (over y_lo, z, core).
Axes of the slice: x: 4, y: 4 (y_hi: 2, y_lo: 2; y = y_hi * 2 + y_lo), z: 4, core: 2. Of those that a mesh axis runs over, the one named last changes fastest.
Arguments:
- tokens: bfloat16 [4096, 4096], P('seq', 'tensor'), may hold values from -6 to 6
- seg_starts: int32 [8], replicated, may hold values from 0 to 4095, as said below
- gain_hyena: float32 [4096], replicated, may hold values from 0.1 to 1.9
- w_hyena_in: bfloat16 [4096, 3, 4096], P(None, None, 'tensor'), may hold values from -0.09375 to 0.09375
- hyena_filter: float32 [128, 4096], P(None, 'tensor'), may hold values from -1 to 1
- w_hyena_out: bfloat16 [4096, 4096], P('tensor'), may hold values from -0.125 to 0.125
- gain_attn: float32 [4096], replicated, may hold values from 0.1 to 1.9
- w_attn_in: bfloat16 [4096, 3, 4096], P(None, None, 'tensor'), may hold values from -0.75 to 0.75
- w_attn_out: bfloat16 [4096, 4096], P('tensor'), may hold values from -0.125 to 0.125
Outputs:
- block_out: float32 [4096, 4096], P('seq', 'tensor')
The draws below stay inside these ranges and needn't reach their ends.
Inputs may be any that keep to these rules, and one draw needn't show every extreme that they name: Ascending and distinct, the first is 0, every other one at or after 4096 - 4096 // 4; genome i runs from seg_starts[i] to the next start, the last to the end of the window.
All inputs are finite; a program needn't handle non-finite values.
Results may differ from the reference program's by a relative error of at most 0.0079.
Values may be sent and summed in bfloat16 or wider, within the bound.
No kernel may reach another device: no remote copies, remote signals or barrier semaphores. Data moves between devices by JAX's collectives and lax.ppermute only.
A program may use at most 128 MiB of HBM per device.

```python
import jax
import jax.numpy as jnp
from jax import lax

HEADS = 32
HD = 128
D = 4096
FILT = 128
SEGS = 8
WINDOW = 4096


def draw_seg_starts(key, part):
    key = jax.random.fold_in(key, 5)
    quarter = WINDOW // 4
    picks = jax.random.permutation(key, quarter)[:SEGS - 1] + (WINDOW - quarter)
    first = jnp.zeros((1,), jnp.int32)
    return jnp.concatenate([first, jnp.sort(picks.astype(jnp.int32))]).astype(jnp.int32)


def draw_hyena_filter(key, part):
    key = jax.random.fold_in(key, 11)
    reach_key, base_key = jax.random.split(key)
    taps = jnp.arange(FILT, dtype=jnp.float32)
    reach = jnp.exp(jax.random.uniform(reach_key, (D,), jnp.float32, jnp.log(FILT / 4.0), jnp.log(FILT * 4.0)))
    base = jax.random.truncated_normal(base_key, -6.0, 6.0, (FILT, D), jnp.float32)
    return (0.15 * base * jnp.exp(-taps[:, None] / reach[None, :])).astype(jnp.float32)


def draw_w_attn_in(key, part):
    key = jax.random.fold_in(key, 23)
    base_key = jax.random.fold_in(key, 0)
    base = jax.random.truncated_normal(base_key, -6.0, 6.0, (D, 3, D), jnp.float32) / jnp.sqrt(D * 1.0)
    return base.astype(jnp.bfloat16)


def spiked(drawn, rng, source, target, blocks, factor):
    owner, partner = [(jnp.arange(drawn.shape[position]) // (drawn.shape[position] // blocks)).reshape([-1 if axis == position else 1 for axis in range(drawn.ndim)]) for position in (source, target)]
    chosen = jax.random.permutation(rng, blocks)[partner]
    strong = (owner == chosen) | (owner == (partner + blocks // 2) % blocks)
    return jnp.where(strong, factor * drawn, drawn)


def block_scale(key, shape, cuts, least, top_value):
    def one(dim, parts):
        draws = jax.random.uniform(jax.random.fold_in(jax.random.fold_in(key, 6), dim), (parts,), jnp.float32, least / len(cuts), top_value / len(cuts))
        return jnp.repeat(jnp.exp(draws), shape[dim] // parts).reshape((-1,) + (1,) * (len(shape) - dim - 1))

    level = one(*cuts[0])
    for cut in cuts[1:]:
        level = level * one(*cut)
    return level


def scatter_about(key, dims, spread, most, pieces=(), kind=jnp.bfloat16):
    level = block_scale(key, dims, pieces, -0.22, 0.18) if pieces else 1.0
    result = jax.random.normal(key, dims, jnp.float32) * spread * level
    return jnp.minimum(jnp.maximum(result, -most), most).astype(kind)


def heavy_noise(own_key, extent, width, most, shards, heavy, kind=jnp.bfloat16):
    array = width * jax.random.normal(own_key, extent, jnp.float32)
    if shards:
        array = array * block_scale(own_key, extent, shards, -0.22, 0.18)
    return jnp.clip(spiked(array, jax.random.fold_in(own_key, 3), *heavy), -most, most).astype(kind)


def setup_inputs(seed: int = 0) -> dict:
    streams_of = jax.random.split(jax.random.key(seed), 10)
    return {
        "tokens": scatter_about(streams_of[0], (WINDOW, D), 1.0, 6.0, ((0, 8), (1, 16))),
        "seg_starts": draw_seg_starts(jax.random.fold_in(streams_of[9], 71), 0),
        "gain_hyena": jnp.clip(1.0 + 0.18 * jax.random.normal(streams_of[2], (D,), jnp.float32), 0.1, 1.9),
        "w_hyena_in": scatter_about(streams_of[3], (D, 3, D), D ** -0.5, 0.09375, ((2, 16),)),
        "hyena_filter": draw_hyena_filter(jax.random.fold_in(streams_of[9], 71), 0),
        "w_hyena_out": heavy_noise(streams_of[5], (D, D), D ** -0.5, 0.125, ((0, 16),), (0, 1, 16, 2.0)),
        "gain_attn": jnp.clip(1.0 + 0.18 * jax.random.normal(streams_of[6], (D,), jnp.float32), 0.1, 1.9),
        "w_attn_in": draw_w_attn_in(jax.random.fold_in(streams_of[9], 71), 0),
        "w_attn_out": heavy_noise(streams_of[8], (D, D), D ** -0.5, 0.125, ((0, 16),), (0, 1, 16, 2.0)),
    }


def rms_scale(values, gain):
    wide = values.astype(jnp.float32)
    factor = lax.rsqrt(lax.optimization_barrier(jnp.mean(wide * wide, axis=-1, keepdims=True)) + 1e-05)
    return (wide * factor * gain).astype(jnp.bfloat16)

def segment_begin(positions, seg_starts):
    below = seg_starts[None, :] <= positions[:, None]
    return lax.optimization_barrier(jnp.max(jnp.where(below, seg_starts[None, :], 0), axis=1)).astype(jnp.int32)

def rotate(heads_in, positions):
    half_dim = heads_in.shape[-1] // 2
    freqs = 10000.0 ** (-2.0 * jnp.arange(half_dim, dtype=jnp.float32) / heads_in.shape[-1])
    angles = positions.astype(jnp.float32)[:, None] * freqs[None, :]
    cosine = jnp.cos(angles)[:, None, :]
    sine = jnp.sin(angles)[:, None, :]
    wide = heads_in.astype(jnp.float32)
    first = wide[..., :half_dim]
    second = wide[..., half_dim:]
    joined = jnp.concatenate([first * cosine - second * sine, second * cosine + first * sine], axis=-1)
    return joined.astype(jnp.bfloat16)

def filter_conv(extended, taps, reach):
    length = taps.shape[0]
    out_rows = extended.shape[0] - (length - 1)

    def tap_step(index, running):
        begin = (length - 1 - index).astype(jnp.int32)
        window_rows = lax.dynamic_slice_in_dim(extended, begin, out_rows, 0)
        keep = (index <= reach)[:, None]
        return running + jnp.where(keep, taps[index][None, :] * window_rows, 0.0)
    start_value = jnp.zeros((out_rows, extended.shape[1]), jnp.float32)
    return lax.fori_loop(0, length, tap_step, start_value)

def attend_head(query, keys, values, positions, begins):
    scores = jnp.dot(query, keys.T, preferred_element_type=jnp.float32) * query.shape[-1] ** (-0.5)
    allowed = (positions[None, :] <= positions[:, None]) & (positions[None, :] >= begins[:, None])
    scores = jnp.where(allowed, scores, -jnp.inf)
    peak = lax.optimization_barrier(jnp.max(scores, axis=1, keepdims=True))
    weights = jnp.exp(scores - peak)
    total = lax.optimization_barrier(jnp.sum(weights, axis=1, keepdims=True))
    return jnp.dot(weights.astype(jnp.bfloat16), values, preferred_element_type=jnp.float32) / total

def reference(tokens, seg_starts, gain_hyena, w_hyena_in, hyena_filter, w_hyena_out, gain_attn, w_attn_in, w_attn_out):
    positions = jnp.arange(WINDOW, dtype=jnp.int32)
    begins = segment_begin(positions, seg_starts)
    normed = rms_scale(tokens, gain_hyena)
    streams = jnp.dot(normed, w_hyena_in.reshape(D, 3 * D), preferred_element_type=jnp.float32)
    streams = streams.astype(jnp.bfloat16).reshape(WINDOW, 3, D)
    product = (streams[:, 1].astype(jnp.float32) * streams[:, 2].astype(jnp.float32)).astype(jnp.bfloat16)
    extended = jnp.concatenate([jnp.zeros((FILT - 1, D), jnp.float32), product.astype(jnp.float32)], axis=0)
    convolved = filter_conv(extended, hyena_filter, positions - begins)
    gated = (streams[:, 0].astype(jnp.float32) * convolved).astype(jnp.bfloat16)
    middle = tokens.astype(jnp.float32) + jnp.dot(gated, w_hyena_out, preferred_element_type=jnp.float32)
    normed_attn = rms_scale(middle, gain_attn)
    projected = jnp.dot(normed_attn, w_attn_in.reshape(D, 3 * D), preferred_element_type=jnp.float32)
    projected = projected.astype(jnp.bfloat16).reshape(WINDOW, 3, HEADS, HD)
    queries = rotate(projected[:, 0], positions)
    keys = rotate(projected[:, 1], positions)
    values = projected[:, 2]

    def per_head(trio):
        return attend_head(trio[0], trio[1], trio[2], positions, begins)
    context = lax.map(per_head, (queries.transpose(1, 0, 2), keys.transpose(1, 0, 2), values.transpose(1, 0, 2)))
    context = context.transpose(1, 0, 2).reshape(WINDOW, D).astype(jnp.bfloat16)
    return middle + jnp.dot(context, w_attn_out, preferred_element_type=jnp.float32)
```

```python
import functools
import math

import jax
import jax.numpy as jnp
from jax import lax
from jax.experimental import pallas as pl
from jax.experimental.pallas import tpu as pltpu
from jax.sharding import PartitionSpec as P

HD = 128
TAPS = 128
BF = jnp.bfloat16
F32 = jnp.float32
NEG = -1e30
VMEM = pl.BlockSpec(memory_space=pltpu.VMEM)
SMEM = pl.BlockSpec(memory_space=pltpu.SMEM)
LIMIT = 40 * 2**20


def tensor_route(move):
    pairs = []
    for t in range(16):
        y, z, c = move(t // 8, t // 2 % 4, t % 2)
        pairs.append((t, (y % 2) * 8 + (z % 4) * 2 + c % 2))
    return pairs


ROUTE_Y = tensor_route(lambda y, z, c: (y + 1, z, c))
ROUTE_UP = tensor_route(lambda y, z, c: (y, z + 1, c))
ROUTE_DOWN = tensor_route(lambda y, z, c: (y, z - 1, c))
ROUTE_FAR = tensor_route(lambda y, z, c: (y, z + 2, c))
ROUTE_CORE = tensor_route(lambda y, z, c: (y, z, c + 1))


def send(block, route, axis="tensor"):
    return lax.ppermute(block, axis, route)


def gather_tensor(block):
    side = send(block, ROUTE_Y)
    below = send(block, ROUTE_UP)
    above = send(block, ROUTE_DOWN)
    far = send(block, ROUTE_FAR)
    side_below = send(side, ROUTE_UP)
    side_above = send(side, ROUTE_DOWN)
    side_far = send(far, ROUTE_Y)
    mine = [block, above, far, below, side, side_above, side_far, side_below]
    return mine + [send(one, ROUTE_CORE) for one in mine]


EARLY = [0, 8, 4, 12, 1, 9, 3, 11]
LATE = [2, 10, 5, 13, 7, 15, 6, 14]


def relative_order(position):
    y, z, c = position // 8, position // 2 % 4, position % 2
    out = []
    for dc in range(2):
        for dy in range(2):
            for dz in range(4):
                out.append(((y + dy) % 2) * 8 + ((z + dz) % 4) * 2 + (c + dc) % 2)
    return jnp.stack(out).astype(jnp.int32)


def scatter_tensor(mine, other):
    received = send(other, ROUTE_CORE)

    def part(i):
        return (mine[i].astype(F32) + received[i].astype(F32)).astype(BF)

    side = send(part(6), ROUTE_Y)
    up = send(jnp.stack([part(1), part(5)]), ROUTE_UP)
    down = send(jnp.stack([part(3), part(7)]), ROUTE_DOWN)
    two = (mine[2].astype(F32) + received[2].astype(F32) + side.astype(F32)).astype(BF)
    far = send(two, ROUTE_FAR)
    across = mine[4].astype(F32) + received[4].astype(F32) + up[1].astype(F32) + down[1].astype(F32)
    back = send(across.astype(BF), ROUTE_Y)
    near = mine[0].astype(F32) + received[0].astype(F32) + up[0].astype(F32) + down[0].astype(F32)
    return near + far.astype(F32) + back.astype(F32)


def project_kernel(epilogue, count, carried, order, *refs):
    refs = list(refs)
    blocks = [refs.pop(0) for _ in range(count)]
    gain = refs.pop(0)
    weight = refs.pop(0)
    sums_in, square_in = (refs.pop(0), refs.pop(0)) if carried else (None, None)
    tables = (refs.pop(0), refs.pop(0)) if epilogue == "rotate" or epilogue == "keys" else None
    scaled = refs.pop()
    square = refs.pop()
    outs = refs
    step = pl.program_id(0)

    @pl.when(step == 0)
    def _():
        total = None
        for k in range(count):
            wide = blocks[k][...].astype(F32)
            scaled[k] = (wide * gain[order[k]]).astype(BF)
            part = wide * wide
            total = part if total is None else total + part
        total = jnp.sum(total, axis=1, keepdims=True)
        if carried:
            total = total + square_in[...]
        square[...] = total

    acc = sums_in[0] if carried else None
    for k in range(count):
        term = jnp.dot(scaled[k], weight[0, order[k]], preferred_element_type=F32)
        acc = term if acc is None else acc + term
    if epilogue == "sums":
        outs[0][0] = acc
        outs[1][...] = square[...]
        return
    width = 16 * acc.shape[1]
    acc = acc * lax.rsqrt(square[...] / width + 1e-05)
    half = acc.astype(BF)

    def rotated():
        cosine, sine = tables
        parts = []
        for h in range(half.shape[1] // HD):
            head = half[:, h * HD : (h + 1) * HD].astype(F32)
            turned = pltpu.roll(head, HD // 2, 1)
            parts.append((head * cosine[...] + turned * sine[...]).astype(BF))
        return jnp.concatenate(parts, axis=1)

    if epilogue == "plain":
        outs[0][...] = half
    elif epilogue == "rotate":
        outs[0][...] = rotated()
    elif epilogue == "product":

        @pl.when(step == 0)
        def _():
            outs[0][...] = half

        @pl.when(step == 1)
        def _():
            outs[0][...] = (outs[0][...].astype(F32) * half.astype(F32)).astype(BF)

    else:
        width = half.shape[1]

        @pl.when(step == 0)
        def _():
            outs[0][:, 0:width] = rotated()

        @pl.when(step == 1)
        def _():
            outs[0][:, width : 2 * width] = half


def project(epilogue, blocks, order, gain, weight, first, steps, carry=None, tables=None):
    rows, wide = blocks[0].shape
    cols = weight.shape[3]
    count = len(blocks)

    def whole(shape):
        return pl.BlockSpec(shape, lambda i, o: (0,) * len(shape))

    in_specs = [whole((rows, wide))] * count + [whole(gain.shape)]
    in_specs.append(pl.BlockSpec((1, 16, wide, cols), lambda i, o: (first + i, 0, 0, 0)))
    operands = [*blocks, gain, weight]
    if carry is not None:
        in_specs += [pl.BlockSpec((1, rows, cols), lambda i, o: (first + i, 0, 0)), whole((rows, 1))]
        operands += list(carry)
    if tables is not None:
        in_specs += [whole(tables[0].shape)] * 2
        operands += list(tables)
    if epilogue == "sums":
        out_shape = (jax.ShapeDtypeStruct((steps, rows, cols), F32), jax.ShapeDtypeStruct((rows, 1), F32))
        out_specs = (pl.BlockSpec((1, rows, cols), lambda i, o: (i, 0, 0)), whole((rows, 1)))
    else:
        out_cols = 2 * cols if epilogue == "keys" else cols
        out_shape = jax.ShapeDtypeStruct((rows, out_cols), BF)
        out_specs = whole((rows, out_cols))
    return pl.pallas_call(
        functools.partial(project_kernel, epilogue, count, carry is not None),
        out_shape=out_shape,
        grid_spec=pltpu.PrefetchScalarGridSpec(
            num_scalar_prefetch=1,
            grid=(steps,),
            in_specs=in_specs,
            out_specs=out_specs,
            scratch_shapes=[pltpu.VMEM((rows, 1), F32), pltpu.VMEM((count, rows, wide), BF)],
        ),
        compiler_params=pltpu.CompilerParams(vmem_limit_bytes=LIMIT),
        cost_estimate=pl.CostEstimate(
            flops=2 * rows * wide * count * cols * steps,
            bytes_accessed=2 * (rows * wide * count + wide * 16 * cols * steps + 2 * rows * cols),
            transcendentals=0,
        ),
        name=f"project_{epilogue}",
    )(order, *operands)


def spread_kernel(order, x, weight, out):
    wide = out.shape[2]
    for k in range(out.shape[0]):
        columns = pl.ds(pl.multiple_of(order[k] * wide, wide), wide)
        out[k] = jnp.dot(x[...], weight[:, columns], preferred_element_type=F32).astype(BF)


def spread(x, weight, order):
    rows, wide = x.shape
    count = order.shape[0]
    return pl.pallas_call(
        spread_kernel,
        out_shape=jax.ShapeDtypeStruct((count, rows, wide), BF),
        in_specs=[SMEM, VMEM, VMEM],
        out_specs=VMEM,
        compiler_params=pltpu.CompilerParams(vmem_limit_bytes=LIMIT),
        cost_estimate=pl.CostEstimate(
            flops=2 * rows * wide * wide * count,
            bytes_accessed=2 * (rows * wide + wide * wide * count + rows * wide * count),
            transcendentals=0,
        ),
        name="spread",
    )(order, x, weight)


def filter_kernel(tile, extended, taps, reach, gate, out, shifted):
    total = extended.shape[0]
    rows = out.shape[0]
    wide = extended[...].astype(F32)
    shifted[0] = wide
    for r in range(1, 8):
        shifted[r, 8:total] = shifted[0, 8 - r : total - r]

    def row_tile(i, carry):
        base = pl.multiple_of(i * tile, tile)
        limit = jnp.broadcast_to(reach[pl.ds(base, tile), :], (tile, HD))
        parts = out.shape[1] // HD

        def group(a, accs):
            start = pl.multiple_of(base + TAPS - 8 * a, 8)
            tap_rows = taps[pl.ds(pl.multiple_of(8 * a, 8), 8), :]
            accs = list(accs)
            for r in range(8):
                keep = limit >= 8 * a + r
                for p in range(parts):
                    lanes = slice(p * HD, (p + 1) * HD)
                    window = shifted[r, pl.ds(start, tile), lanes]
                    term = tap_rows[r : r + 1, lanes] * window
                    accs[p] = accs[p] + jnp.where(keep, term, 0.0)
            return tuple(accs)

        zero = tuple(jnp.zeros((tile, HD), F32) for _ in range(parts))
        accs = lax.fori_loop(0, TAPS // 8, group, zero)
        for p in range(parts):
            lanes = slice(p * HD, (p + 1) * HD)
            query = gate[pl.ds(base, tile), lanes].astype(F32)
            out[pl.ds(base, tile), lanes] = (query * accs[p]).astype(BF)
        return carry

    lax.fori_loop(0, rows // tile, row_tile, 0)


def filtered(extended, taps, reach, gate):
    rows, width = gate.shape
    return pl.pallas_call(
        functools.partial(filter_kernel, 64),
        out_shape=jax.ShapeDtypeStruct((rows, width), BF),
        in_specs=[VMEM] * 4,
        out_specs=VMEM,
        scratch_shapes=[pltpu.VMEM((8, rows + TAPS, width), F32)],
        compiler_params=pltpu.CompilerParams(vmem_limit_bytes=LIMIT),
        cost_estimate=pl.CostEstimate(
            flops=6 * TAPS * rows * width * 40, bytes_accessed=8 * rows * width, transcendentals=0
        ),
        name="filtered",
    )(extended, taps, reach, gate)


def attend_kernel(last, width, me_ref, q_ref, begin_ref, *refs):
    refs = list(refs)
    pieces = [refs.pop(0) for _ in range(4)]
    if last:
        before = [refs.pop(0) for _ in range(3)]
        (out,) = refs[:1]
        peak, total, running = refs[1:]
    else:
        peak, total, running = refs
    me = me_ref[0]
    rows = q_ref.shape[0]
    heads = width // HD
    chunk = 128
    scale = HD**-0.5 * math.log2(math.e)
    x = me % 4
    row_block = me // 4
    if last:
        peak[...] = before[0][...]
        total[...] = before[1][...]
        running[...] = before[2][...]
    else:
        peak[...] = jnp.full(peak.shape, NEG, F32)
        total[...] = jnp.zeros(total.shape, F32)
        running[...] = jnp.zeros(running.shape, F32)
    for i, dx in enumerate((0, 3, 1, 2)):
        owner = (row_block - 1 if last else row_block) * 4 + (x + dx) % 4

        @pl.when((row_block > 0) if last else (owner <= me))
        def _(i=i, owner=owner):
            piece = pieces[i]

            def one(step, carry):
                base = pl.multiple_of(step * chunk, chunk)
                span = pl.ds(base, chunk)
                begin = begin_ref[span, :]
                if last:
                    open_row = begin <= owner * rows
                else:
                    key_at = owner * rows + lax.broadcasted_iota(jnp.int32, (chunk, rows), 1)
                    row_at = me * rows + base + lax.broadcasted_iota(jnp.int32, (chunk, rows), 0)
                    allowed = (key_at <= row_at) & (key_at >= begin)
                for h in range(heads):
                    lanes = slice(h * HD, (h + 1) * HD)
                    keys = piece[:, lanes]
                    values = piece[:, width + h * HD : width + (h + 1) * HD]
                    scores = lax.dot_general(
                        q_ref[span, lanes], keys, (((1,), (1,)), ((), ())), preferred_element_type=F32
                    )
                    old = peak[h, span, :]
                    if last:
                        top = jnp.max(scores, axis=1, keepdims=True)
                        new = jnp.where(open_row, jnp.maximum(old, top), old)
                        level = jnp.where(open_row, new, -NEG)
                    else:
                        scores = jnp.where(allowed, scores, NEG)
                        new = jnp.maximum(old, jnp.max(scores, axis=1, keepdims=True))
                        level = new
                    weights = jnp.exp2((scores - level) * scale)
                    factor = jnp.exp2((old - new) * scale)
                    peak[h, span, :] = new
                    total[h, span, :] = total[h, span, :] * factor + jnp.sum(weights, axis=1, keepdims=True)
                    update = jnp.dot(weights.astype(BF), values, preferred_element_type=F32)
                    running[h, span, :] = running[h, span, :] * factor + update
                return carry

            lax.fori_loop(0, rows // chunk, one, 0)

    if last:
        for h in range(heads):
            out[:, h * HD : (h + 1) * HD] = (running[h] / total[h]).astype(BF)


def attend(me, queries, begins, pieces, before=None):
    rows, width = queries.shape
    heads = width // HD
    state = [(heads, rows, 1), (heads, rows, 1), (heads, rows, HD)]
    last = before is not None
    if last:
        out_shape = jax.ShapeDtypeStruct((rows, width), BF)
        scratch = [pltpu.VMEM(s, F32) for s in state]
        out_specs = VMEM
    else:
        out_shape = tuple(jax.ShapeDtypeStruct(s, F32) for s in state)
        scratch = []
        out_specs = (VMEM,) * 3
    before = tuple(before) if last else ()
    return pl.pallas_call(
        functools.partial(attend_kernel, last, width),
        out_shape=out_shape,
        in_specs=[SMEM] + [VMEM] * (2 + 4 + len(before)),
        out_specs=out_specs,
        scratch_shapes=scratch,
        compiler_params=pltpu.CompilerParams(vmem_limit_bytes=LIMIT),
        cost_estimate=pl.CostEstimate(
            flops=4 * rows * rows * width * 4 * 3, bytes_accessed=2 * 10 * rows * width, transcendentals=rows * rows * 8
        ),
        name="attend_far" if last else "attend_near",
    )(me, queries, begins, *pieces, *before)


def row_ring(piece, lines):
    full = lines == (1,)

    def route(pairs):
        return [(y * 4 + a, y * 4 + b) for y in lines for a, b in pairs]

    up = [(0, 1), (1, 2), (2, 3)] + ([(3, 0)] if full else [])
    down = [(0, 3), (1, 0)] + ([(2, 1), (3, 2)] if full else [])
    up_half = [(1, 2), (2, 3)] + ([(3, 0), (0, 1)] if full else [])
    down_half = [(3, 2), (0, 3)] + ([(1, 0), (2, 1)] if full else [])
    half = piece.shape[0] // 2
    left = send(piece, route(up), "seq")
    right = send(piece, route(down), "seq")
    far = jnp.concatenate(
        [send(left[:half], route(up_half), "seq"), send(right[half:], route(down_half), "seq")], axis=0
    )
    return [piece, left, right, far]


def segment_begin(positions, seg_starts):
    below = seg_starts[None, :] <= positions[:, None]
    return jnp.max(jnp.where(below, seg_starts[None, :], 0), axis=1)


def rotation_tables(positions):
    half_dim = HD // 2
    freqs = 10000.0 ** (-2.0 * jnp.arange(half_dim, dtype=F32) / HD)
    angles = positions.astype(F32)[:, None] * freqs[None, :]
    cosine = jnp.cos(angles)
    sine = jnp.sin(angles)
    return jnp.concatenate([cosine, cosine], axis=1), jnp.concatenate([-sine, sine], axis=1)


def shards(
    tokens,
    seg_starts,
    gain_hyena,
    w_hyena_in,
    hyena_filter,
    w_hyena_out,
    gain_attn,
    w_attn_in,
    w_attn_out,
):
    rows, width = tokens.shape
    me = lax.axis_index("seq").astype(jnp.int32)
    order = relative_order(lax.axis_index("tensor"))
    early = order[jnp.array(EARLY)]
    late = order[jnp.array(LATE)]
    positions = me * rows + jnp.arange(rows, dtype=jnp.int32)
    begins = segment_begin(positions, seg_starts)
    reach = (positions - begins)[:, None]
    begins = begins[:, None]
    tables = rotation_tables(positions)

    def streams_of(block, gain, weight, kinds, tables=None):
        blocks = gather_tensor(block)
        gain = gain.reshape(16, 1, width)
        weight = weight.reshape(16, width, 3, width).transpose(2, 0, 1, 3)
        carry = project("sums", [blocks[i] for i in EARLY], early, gain, weight, 0, 3)
        rest = [blocks[i] for i in LATE]
        back = project(kinds[0], rest, late, gain, weight, 1, 2, carry, tables)
        front = project(kinds[1], rest, late, gain, weight, 0, 1, carry, tables)
        return front, back

    def summed_over_tensor(values, weight):
        other = spread(values, weight, order[8:])
        return scatter_tensor(spread(values, weight, order[:8]), other)

    gate, product = streams_of(tokens, gain_hyena, w_hyena_in, ("product", "plain"))
    rim = send(product[rows - TAPS :], [(i, i + 1) for i in range(7)], "seq")
    tail = filtered(product, hyena_filter, reach[TAPS:], gate[TAPS:])
    head = filtered(
        jnp.concatenate([rim, product[:TAPS]], axis=0), hyena_filter, reach[:TAPS], gate[:TAPS]
    )
    gated = jnp.concatenate([head, tail], axis=0)
    middle = tokens.astype(F32) + summed_over_tensor(gated, w_hyena_out)
    queries, own = streams_of(middle.astype(BF), gain_attn, w_attn_in, ("keys", "rotate"), tables)
    below = send(own, [(x, 4 + x) for x in range(4)], "seq")
    near = row_ring(own, (0, 1))
    far = row_ring(below, (1,))
    where = me[None]
    state = attend(where, queries, begins, near)
    context = attend(where, queries, begins, far, state)
    return middle + summed_over_tensor(context, w_attn_out)


def solution(mesh):
    placed = (
        P("seq", "tensor"),
        P(),
        P(),
        P(None, None, "tensor"),
        P(None, "tensor"),
        P("tensor", None),
        P(),
        P(None, None, "tensor"),
        P("tensor", None),
    )
    return jax.shard_map(
        shards, mesh=mesh, in_specs=placed, out_specs=P("seq", "tensor"), check_vma=False
    )
```

```python
import functools
import math

import jax
import jax.numpy as jnp
from jax import lax
from jax.experimental import pallas as pl
from jax.experimental.pallas import tpu as pltpu
from jax.sharding import PartitionSpec as P

HD = 128
TAPS = 128
BF = jnp.bfloat16
F32 = jnp.float32
NEG = -1e30
VMEM = pl.BlockSpec(memory_space=pltpu.VMEM)
SMEM = pl.BlockSpec(memory_space=pltpu.SMEM)
LIMIT = 10 * 2**20
EXTRA = 16


def tensor_route(move):
    pairs = []
    for t in range(16):
        y, z, c = move(t // 8, t // 2 % 4, t % 2)
        pairs.append((t, (y % 2) * 8 + (z % 4) * 2 + c % 2))
    return pairs


ROUTE_Y = tensor_route(lambda y, z, c: (y + 1, z, c))
ROUTE_UP = tensor_route(lambda y, z, c: (y, z + 1, c))
ROUTE_DOWN = tensor_route(lambda y, z, c: (y, z - 1, c))
ROUTE_FAR = tensor_route(lambda y, z, c: (y, z + 2, c))
ROUTE_CORE = tensor_route(lambda y, z, c: (y, z, c + 1))


def send(block, route, axis="tensor"):
    return lax.ppermute(block, axis, route)


def gather_tensor(block):
    side = send(block, ROUTE_Y)
    below = send(block, ROUTE_UP)
    above = send(block, ROUTE_DOWN)
    far = send(block, ROUTE_FAR)
    side_below = send(side, ROUTE_UP)
    side_above = send(side, ROUTE_DOWN)
    side_far = send(far, ROUTE_Y)
    mine = [block, above, far, below, side, side_above, side_far, side_below]
    return mine + [send(one, ROUTE_CORE) for one in mine]


def with_squares(values):
    rows, width = values.shape
    square = jnp.sum(values * values, axis=1).reshape(rows // width, width)
    pieces = []
    for _ in range(3):
        piece = lax.reduce_precision(square, 8, 7)
        pieces.append(piece)
        square = square - piece
    pieces.append(jnp.zeros((EXTRA - 3 * (rows // width), width), F32))
    return jnp.concatenate([values, *pieces], axis=0).astype(BF)


def relative_order(position):
    y, z, c = position // 8, position // 2 % 4, position % 2
    out = []
    for dc in range(2):
        for dy in range(2):
            for dz in range(4):
                out.append(((y + dy) % 2) * 8 + ((z + dz) % 4) * 2 + (c + dc) % 2)
    return jnp.stack(out).astype(jnp.int32)


def scatter_tensor(mine, other):
    received = send(other, ROUTE_CORE)

    def part(i):
        return (mine[i].astype(F32) + received[i].astype(F32)).astype(BF)

    side = send(part(6), ROUTE_Y)
    up = send(part(5), ROUTE_UP)
    down = send(part(7), ROUTE_DOWN)
    two = (mine[2].astype(F32) + received[2].astype(F32) + side.astype(F32)).astype(BF)
    across = mine[4].astype(F32) + received[4].astype(F32) + up.astype(F32) + down.astype(F32)
    two, across, above, below = lax.optimization_barrier((two, across.astype(BF), part(1), part(3)))
    back = send(across, ROUTE_Y)
    far = send(two, ROUTE_FAR)
    up = send(above, ROUTE_UP)
    down = send(below, ROUTE_DOWN)
    near = mine[0].astype(F32) + received[0].astype(F32) + up.astype(F32) + down.astype(F32)
    return near + far.astype(F32) + back.astype(F32)


def project_kernel(streams, kind, order, *refs):
    blocks, (gain, weight), refs = refs[:16], refs[16:18], refs[18:]
    if kind == "attn":
        cosine, sine = refs[:2]
        refs = refs[2:]
    outs, (scaled, held, sems) = refs[:-3], refs[-3:]
    copies = [
        pltpu.make_async_copy(weight.at[j], held.at[n], sems.at[n]) for n, j in enumerate(streams)
    ]
    for copy in copies:
        copy.start()
    width = blocks[0].shape[1]
    rows = blocks[0].shape[0] - EXTRA
    parts = rows // width
    square = sum(block[rows : rows + EXTRA, :].astype(F32) for block in blocks)
    square = square[0:parts] + square[parts : 2 * parts] + square[2 * parts : 3 * parts]
    square = jnp.concatenate([square, jnp.zeros((8 - parts, width), F32)], axis=0)
    factor = lax.rsqrt(square / (16 * width) + 1e-05).T
    for k in range(16):
        columns = pl.ds(pl.multiple_of(order[k] * width, width), width)
        for p in range(parts):
            span = slice(p * width, (p + 1) * width)
            wide = blocks[k][span, :].astype(F32)
            scaled[span, columns] = (wide * factor[:, p : p + 1] * gain[order[k]]).astype(BF)
    halves = []
    for n in range(len(streams)):
        copies[n].wait()
        halves.append(jnp.dot(scaled[...], held[n], preferred_element_type=F32).astype(BF))

    def rotated(half):
        done = []
        for h in range(width // HD):
            head = half[:, h * HD : (h + 1) * HD].astype(F32)
            turned = pltpu.roll(head, HD // 2, 1)
            done.append((head * cosine[...] + turned * sine[...]).astype(BF))
        return jnp.concatenate(done, axis=1)

    if kind == "hyena":
        outs[0][...] = (halves[0].astype(F32) * halves[1].astype(F32)).astype(BF)
        outs[1][...] = halves[2]
    elif len(streams) == 2:
        outs[0][:, 0:width] = rotated(halves[0])
        outs[0][:, width : 2 * width] = halves[1]
    else:
        outs[0][...] = rotated(halves[0])


def project(streams, kind, blocks, order, gain, weight, tables=()):
    rows, width = blocks[0].shape[0] - EXTRA, blocks[0].shape[1]
    features = 16 * width
    count = len(streams)
    if kind == "hyena":
        out_shape = tuple(jax.ShapeDtypeStruct((rows, width), BF) for _ in range(2))
    else:
        out_shape = (jax.ShapeDtypeStruct((rows, count * width), BF),)
    return pl.pallas_call(
        functools.partial(project_kernel, streams, kind),
        out_shape=out_shape,
        in_specs=[SMEM] + [VMEM] * 17 + [pl.BlockSpec(memory_space=pltpu.HBM)] + [VMEM] * len(tables),
        out_specs=(VMEM,) * len(out_shape),
        scratch_shapes=[
            pltpu.VMEM((rows, features), BF),
            pltpu.VMEM((count, features, width), BF),
            pltpu.SemaphoreType.DMA((count,)),
        ],
        compiler_params=pltpu.CompilerParams(vmem_limit_bytes=22 * 2**20),
        cost_estimate=pl.CostEstimate(
            flops=2 * rows * features * width * count,
            bytes_accessed=2 * features * (rows + count * width),
            transcendentals=0,
        ),
        name=f"project_{kind}",
    )(order, *blocks, gain, weight, *tables)


def spread_kernel(order, x, weight, out):
    wide = out.shape[2]
    for k in range(out.shape[0]):
        columns = pl.ds(pl.multiple_of(order[k] * wide, wide), wide)
        out[k] = jnp.dot(x[...], weight[:, columns], preferred_element_type=F32).astype(BF)


def spread(x, weight, order):
    rows, wide = x.shape
    count = order.shape[0]
    return pl.pallas_call(
        spread_kernel,
        out_shape=jax.ShapeDtypeStruct((count, rows, wide), BF),
        in_specs=[SMEM, VMEM, VMEM],
        out_specs=VMEM,
        compiler_params=pltpu.CompilerParams(vmem_limit_bytes=LIMIT),
        cost_estimate=pl.CostEstimate(
            flops=2 * rows * wide * wide * count,
            bytes_accessed=2 * (rows * wide + wide * wide * count + rows * wide * count),
            transcendentals=0,
        ),
        name="spread",
    )(order, x, weight)


def filter_kernel(tile, extended, taps, reach, gate, out, shifted):
    total = extended.shape[0]
    rows = out.shape[0]
    wide = extended[...].astype(F32)
    shifted[0] = wide
    for r in range(1, 8):
        shifted[r, 8:total] = shifted[0, 8 - r : total - r]

    def row_tile(i, carry):
        base = pl.multiple_of(i * tile, tile)
        limit = jnp.broadcast_to(reach[pl.ds(base, tile), :], (tile, HD))
        parts = out.shape[1] // HD

        def group(a, accs):
            start = pl.multiple_of(base + TAPS - 8 * a, 8)
            tap_rows = taps[pl.ds(pl.multiple_of(8 * a, 8), 8), :]
            accs = list(accs)
            for r in range(8):
                keep = limit >= 8 * a + r
                for p in range(parts):
                    lanes = slice(p * HD, (p + 1) * HD)
                    window = shifted[r, pl.ds(start, tile), lanes]
                    term = tap_rows[r : r + 1, lanes] * window
                    accs[p] = accs[p] + jnp.where(keep, term, 0.0)
            return tuple(accs)

        zero = tuple(jnp.zeros((tile, HD), F32) for _ in range(parts))
        accs = lax.fori_loop(0, TAPS // 8, group, zero)
        for p in range(parts):
            lanes = slice(p * HD, (p + 1) * HD)
            query = gate[pl.ds(base, tile), lanes].astype(F32)
            out[pl.ds(base, tile), lanes] = (query * accs[p]).astype(BF)
        return carry

    lax.fori_loop(0, rows // tile, row_tile, 0)


def filtered(extended, taps, reach, gate):
    rows, width = gate.shape
    return pl.pallas_call(
        functools.partial(filter_kernel, 64),
        out_shape=jax.ShapeDtypeStruct((rows, width), BF),
        in_specs=[VMEM] * 4,
        out_specs=VMEM,
        scratch_shapes=[pltpu.VMEM((8, rows + TAPS, width), F32)],
        compiler_params=pltpu.CompilerParams(vmem_limit_bytes=LIMIT),
        cost_estimate=pl.CostEstimate(
            flops=6 * TAPS * rows * width * 40, bytes_accessed=8 * rows * width, transcendentals=0
        ),
        name="filtered",
    )(extended, taps, reach, gate)


def attend_kernel(plan, first, last, me_ref, q_ref, begin_ref, *refs):
    refs = list(refs)
    pieces = [refs.pop(0) for _ in plan]
    before = [] if first else [refs.pop(0) for _ in range(3)]
    out = refs.pop(0) if last else None
    peak, total, running = refs
    me = me_ref[0]
    rows, width = q_ref.shape
    heads = width // HD
    chunk = 256
    scale = HD**-0.5 * math.log2(math.e)
    x = me % 4
    line = me // 4
    if first:
        peak[...] = jnp.full(peak.shape, NEG, F32)
        total[...] = jnp.zeros(total.shape, F32)
        running[...] = jnp.zeros(running.shape, F32)
    else:
        for now, then in zip((peak, total, running), before):
            now[...] = then[...]
    for piece, (dline, dx) in zip(pieces, plan):
        owner = (line - dline) * 4 + (x + dx) % 4

        @pl.when((line > 0) if dline else (owner <= me))
        def _(piece=piece, dline=dline, owner=owner):
            for base in range(0, rows, chunk):
                span = slice(base, base + chunk)
                begin = begin_ref[:, span]
                if dline:
                    open_row = begin <= owner * rows
                else:
                    key_at = owner * rows + lax.broadcasted_iota(jnp.int32, (rows, chunk), 0)
                    row_at = me * rows + base + lax.broadcasted_iota(jnp.int32, (1, chunk), 1)
                    allowed = (key_at <= row_at) & (key_at >= begin)
                for h in range(heads):
                    lanes = slice(h * HD, (h + 1) * HD)
                    keys = piece[:, lanes]
                    values = piece[:, width + h * HD : width + (h + 1) * HD]
                    scores = lax.dot_general(
                        keys, q_ref[span, lanes], (((1,), (1,)), ((), ())), preferred_element_type=F32
                    )
                    old = peak[h, :, span]
                    if dline:
                        top = jnp.max(scores, axis=0, keepdims=True)
                        new = jnp.where(open_row, jnp.maximum(old, top), old)
                        level = jnp.where(open_row, new, -NEG)
                    else:
                        scores = jnp.where(allowed, scores, NEG)
                        new = jnp.maximum(old, jnp.max(scores, axis=0, keepdims=True))
                        level = new
                    weights = jnp.exp2((scores - level) * scale)
                    factor = jnp.exp2((old - new) * scale)
                    peak[h, :, span] = new
                    total[h, :, span] = total[h, :, span] * factor + jnp.sum(weights, axis=0, keepdims=True)
                    update = lax.dot_general(
                        values, weights.astype(BF), (((0,), (0,)), ((), ())), preferred_element_type=F32
                    )
                    running[h, :, span] = running[h, :, span] * factor + update

    if last:
        for h in range(heads):
            out[:, h * HD : (h + 1) * HD] = (running[h] / total[h]).T.astype(BF)


def attend(me, queries, begins, plan, pieces, before=None, last=False):
    rows, width = queries.shape
    heads = width // HD
    state = [(heads, 1, rows), (heads, 1, rows), (heads, HD, rows)]
    if last:
        out_shape = jax.ShapeDtypeStruct((rows, width), BF)
        scratch = [pltpu.VMEM(s, F32) for s in state]
        out_specs = VMEM
    else:
        out_shape = tuple(jax.ShapeDtypeStruct(s, F32) for s in state)
        scratch = []
        out_specs = (VMEM,) * 3
    first = before is None
    before = () if first else tuple(before)
    return pl.pallas_call(
        functools.partial(attend_kernel, plan, first, last),
        out_shape=out_shape,
        in_specs=[SMEM] + [VMEM] * (2 + len(pieces) + len(before)),
        out_specs=out_specs,
        scratch_shapes=scratch,
        compiler_params=pltpu.CompilerParams(vmem_limit_bytes=LIMIT),
        cost_estimate=pl.CostEstimate(
            flops=4 * rows * rows * width * len(pieces) * 4,
            bytes_accessed=4 * (1 + len(pieces)) * rows * width,
            transcendentals=rows * rows * heads * len(pieces),
        ),
        name="attend",
    )(me, queries, begins, *pieces, *before)


def row_ring(piece, lines):
    full = lines == (1,)

    def route(pairs):
        return [(y * 4 + a, y * 4 + b) for y in lines for a, b in pairs]

    up = [(0, 1), (1, 2), (2, 3)] + ([(3, 0)] if full else [])
    down = [(0, 3), (1, 0)] + ([(2, 1), (3, 2)] if full else [])
    up_half = [(1, 2), (2, 3)] + ([(3, 0), (0, 1)] if full else [])
    down_half = [(3, 2), (0, 3)] + ([(1, 0), (2, 1)] if full else [])
    half = piece.shape[0] // 2
    left = send(piece, route(up), "seq")
    right = send(piece, route(down), "seq")
    far = jnp.concatenate(
        [send(left[:half], route(up_half), "seq"), send(right[half:], route(down_half), "seq")], axis=0
    )
    return [piece, left, right, far]


def segment_begin(positions, seg_starts):
    below = seg_starts[None, :] <= positions[:, None]
    return jnp.max(jnp.where(below, seg_starts[None, :], 0), axis=1)


def rotation_tables(positions):
    half_dim = HD // 2
    freqs = 10000.0 ** (-2.0 * jnp.arange(half_dim, dtype=F32) / HD)
    angles = positions.astype(F32)[:, None] * freqs[None, :]
    cosine = jnp.cos(angles)
    sine = jnp.sin(angles)
    return jnp.concatenate([cosine, cosine], axis=1), jnp.concatenate([-sine, sine], axis=1)


def shards(
    tokens,
    seg_starts,
    gain_hyena,
    w_hyena_in,
    hyena_filter,
    w_hyena_out,
    gain_attn,
    w_attn_in,
    w_attn_out,
):
    rows, width = tokens.shape
    me = lax.axis_index("seq").astype(jnp.int32)
    order = relative_order(lax.axis_index("tensor"))
    positions = me * rows + jnp.arange(rows, dtype=jnp.int32)
    begins = segment_begin(positions, seg_starts)
    reach = (positions - begins)[:, None]
    begins = begins[None, :]
    tables = rotation_tables(positions)

    def summed_over_tensor(values, weight):
        other = spread(values, weight, order[8:])
        return scatter_tensor(spread(values, weight, order[:8]), other)

    def stacked(weight):
        return weight.transpose(1, 0, 2)

    gain_hyena = gain_hyena.reshape(16, 1, width)
    gain_attn = gain_attn.reshape(16, 1, width)
    blocks = gather_tensor(with_squares(tokens.astype(F32)))
    product, gate = project((1, 2, 0), "hyena", blocks, order, gain_hyena, stacked(w_hyena_in))
    rim = send(product[rows - TAPS :], [(i, i + 1) for i in range(7)], "seq")
    tail = filtered(product, hyena_filter, reach[TAPS:], gate[TAPS:])
    head = filtered(
        jnp.concatenate([rim, product[:TAPS]], axis=0), hyena_filter, reach[:TAPS], gate[:TAPS]
    )
    gated = jnp.concatenate([head, tail], axis=0)
    middle = tokens.astype(F32) + summed_over_tensor(gated, w_hyena_out)
    blocks = gather_tensor(with_squares(middle))
    (own,) = project((1, 2), "attn", blocks, order, gain_attn, stacked(w_attn_in), tables)
    (queries,) = project((0,), "attn", blocks, order, gain_attn, stacked(w_attn_in), tables)
    below = send(own, [(x, 4 + x) for x in range(4)], "seq")
    near = row_ring(own, (0, 1))
    far = row_ring(below, (1,))
    where = me[None]
    state = attend(where, queries, begins, ((0, 0), (0, 3), (0, 1)), near[:3])
    state = attend(where, queries, begins, ((0, 2), (1, 0)), [near[3], far[0]], state)
    context = attend(where, queries, begins, ((1, 3), (1, 1), (1, 2)), far[1:], state, True)
    return middle + summed_over_tensor(context, w_attn_out)


def solution(mesh):
    placed = (
        P("seq", "tensor"),
        P(),
        P(),
        P(None, None, "tensor"),
        P(None, "tensor"),
        P("tensor", None),
        P(),
        P(None, None, "tensor"),
        P("tensor", None),
    )
    return jax.shard_map(
        shards, mesh=mesh, in_specs=placed, out_specs=P("seq", "tensor"), check_vma=False
    )
```

```python
import functools
import math

import jax
import jax.numpy as jnp
from jax import lax
from jax.experimental import pallas as pl
from jax.experimental.pallas import tpu as pltpu
from jax.sharding import PartitionSpec as P

HD = 128
TAPS = 128
BF = jnp.bfloat16
F32 = jnp.float32
NEG = -1e30
VMEM = pl.BlockSpec(memory_space=pltpu.VMEM)
SMEM = pl.BlockSpec(memory_space=pltpu.SMEM)
LIMIT = 10 * 2**20
EXTRA = 16
PROJECT_LIMIT = 46 * 2**20


def tensor_route(move):
    pairs = []
    for t in range(16):
        y, z, c = move(t // 8, t // 2 % 4, t % 2)
        pairs.append((t, (y % 2) * 8 + (z % 4) * 2 + c % 2))
    return pairs


ROUTE_Y = tensor_route(lambda y, z, c: (y + 1, z, c))
ROUTE_UP = tensor_route(lambda y, z, c: (y, z + 1, c))
ROUTE_DOWN = tensor_route(lambda y, z, c: (y, z - 1, c))
ROUTE_FAR = tensor_route(lambda y, z, c: (y, z + 2, c))
ROUTE_CORE = tensor_route(lambda y, z, c: (y, z, c + 1))


def send(block, route, axis="tensor"):
    return lax.ppermute(block, axis, route)


def gather_tensor(block):
    side = send(block, ROUTE_Y)
    below = send(block, ROUTE_UP)
    above = send(block, ROUTE_DOWN)
    far = send(block, ROUTE_FAR)
    side_below = send(side, ROUTE_UP)
    side_above = send(side, ROUTE_DOWN)
    side_far = send(far, ROUTE_Y)
    mine = [block, above, far, below, side, side_above, side_far, side_below]
    return mine + [send(one, ROUTE_CORE) for one in mine]


def with_squares(values):
    rows, width = values.shape
    square = jnp.sum(values * values, axis=1).reshape(rows // width, width)
    pieces = []
    for _ in range(3):
        piece = lax.reduce_precision(square, 8, 7)
        pieces.append(piece)
        square = square - piece
    pieces.append(jnp.zeros((EXTRA - 3 * (rows // width), width), F32))
    return jnp.concatenate([values, *pieces], axis=0).astype(BF)


def relative_order(position):
    y, z, c = position // 8, position // 2 % 4, position % 2
    out = []
    for dc in range(2):
        for dy in range(2):
            for dz in range(4):
                out.append(((y + dy) % 2) * 8 + ((z + dz) % 4) * 2 + (c + dc) % 2)
    return jnp.stack(out).astype(jnp.int32)


def scatter_tensor(mine, other):
    received = send(other, ROUTE_CORE)

    def part(i):
        return (mine[i].astype(F32) + received[i].astype(F32)).astype(BF)

    side = send(part(6), ROUTE_Y)
    up = send(part(5), ROUTE_UP)
    down = send(part(7), ROUTE_DOWN)
    two = (mine[2].astype(F32) + received[2].astype(F32) + side.astype(F32)).astype(BF)
    across = mine[4].astype(F32) + received[4].astype(F32) + up.astype(F32) + down.astype(F32)
    above = send(part(1), ROUTE_UP)
    below = send(part(3), ROUTE_DOWN)
    two, across = lax.optimization_barrier((two, across.astype(BF)))
    back = send(across, ROUTE_Y)
    far = send(two, ROUTE_FAR)
    near = mine[0].astype(F32) + received[0].astype(F32) + above.astype(F32) + below.astype(F32)
    return near + far.astype(F32) + back.astype(F32)


def project_kernel(streams, kind, order, *refs):
    blocks, (gain, weight), refs = refs[:16], refs[16:18], refs[18:]
    if kind == "attn":
        cosine, sine = refs[:2]
        refs = refs[2:]
    outs, (scaled, held, sems) = refs[:-3], refs[-3:]
    copies = [
        pltpu.make_async_copy(
            weight.at[j], held.at[:, pl.ds(n * held.shape[1] // len(streams), held.shape[1] // len(streams))], sems.at[n]
        )
        for n, j in enumerate(streams)
    ]
    for copy in copies:
        copy.start()
    width = blocks[0].shape[1]
    rows = blocks[0].shape[0] - EXTRA
    parts = rows // width
    square = sum(block[rows : rows + EXTRA, :].astype(F32) for block in blocks)
    square = square[0:parts] + square[parts : 2 * parts] + square[2 * parts : 3 * parts]
    square = jnp.concatenate([square, jnp.zeros((8 - parts, width), F32)], axis=0)
    factor = lax.rsqrt(square / (16 * width) + 1e-05).T
    for k in range(16):
        columns = pl.ds(pl.multiple_of(order[k] * width, width), width)
        for p in range(parts):
            span = slice(p * width, (p + 1) * width)
            wide = blocks[k][span, :].astype(F32)
            scaled[span, columns] = (wide * factor[:, p : p + 1] * gain[order[k]]).astype(BF)
    for copy in copies:
        copy.wait()
    whole = jnp.dot(scaled[...], held[...], preferred_element_type=F32).astype(BF)
    halves = [whole[:, n * width : (n + 1) * width] for n in range(len(streams))]

    def rotated(half):
        done = []
        for h in range(width // HD):
            head = half[:, h * HD : (h + 1) * HD].astype(F32)
            turned = pltpu.roll(head, HD // 2, 1)
            done.append((head * cosine[...] + turned * sine[...]).astype(BF))
        return jnp.concatenate(done, axis=1)

    if kind == "hyena":
        outs[0][...] = (halves[0].astype(F32) * halves[1].astype(F32)).astype(BF)
        outs[1][...] = halves[2]
    elif len(streams) == 2:
        outs[0][:, 0:width] = rotated(halves[0])
        outs[0][:, width : 2 * width] = halves[1]
    else:
        outs[0][...] = rotated(halves[0])


def project(streams, kind, blocks, order, gain, weight, tables=()):
    rows, width = blocks[0].shape[0] - EXTRA, blocks[0].shape[1]
    features = 16 * width
    count = len(streams)
    if kind == "hyena":
        out_shape = tuple(jax.ShapeDtypeStruct((rows, width), BF) for _ in range(2))
    else:
        out_shape = (jax.ShapeDtypeStruct((rows, count * width), BF),)
    return pl.pallas_call(
        functools.partial(project_kernel, streams, kind),
        out_shape=out_shape,
        in_specs=[SMEM] + [VMEM] * 17 + [pl.BlockSpec(memory_space=pltpu.HBM)] + [VMEM] * len(tables),
        out_specs=(VMEM,) * len(out_shape),
        scratch_shapes=[
            pltpu.VMEM((rows, features), BF),
            pltpu.VMEM((features, count * width), BF),
            pltpu.SemaphoreType.DMA((count,)),
        ],
        compiler_params=pltpu.CompilerParams(vmem_limit_bytes=PROJECT_LIMIT),
        cost_estimate=pl.CostEstimate(
            flops=2 * rows * features * width * count,
            bytes_accessed=2 * features * (rows + count * width),
            transcendentals=0,
        ),
        name=f"project_{kind}",
    )(order, *blocks, gain, weight, *tables)


def spread_kernel(order, x, weight, out):
    wide = out.shape[2]
    for k in range(out.shape[0]):
        columns = pl.ds(pl.multiple_of(order[k] * wide, wide), wide)
        out[k] = jnp.dot(x[...], weight[:, columns], preferred_element_type=F32).astype(BF)


def spread(x, weight, order):
    rows, wide = x.shape
    count = order.shape[0]
    return pl.pallas_call(
        spread_kernel,
        out_shape=jax.ShapeDtypeStruct((count, rows, wide), BF),
        in_specs=[SMEM, VMEM, VMEM],
        out_specs=VMEM,
        compiler_params=pltpu.CompilerParams(vmem_limit_bytes=LIMIT),
        cost_estimate=pl.CostEstimate(
            flops=2 * rows * wide * wide * count,
            bytes_accessed=2 * (rows * wide + wide * wide * count + rows * wide * count),
            transcendentals=0,
        ),
        name="spread",
    )(order, x, weight)


def filter_kernel(tile, least, most, extended, taps, reach, gate, out, shifted):
    total = extended.shape[0]
    rows = out.shape[0]
    wide = extended[...].astype(F32)
    shifted[0] = wide
    for r in range(1, 8):
        shifted[r, 8:total] = shifted[0, 8 - r : total - r]

    def row_tile(i, carry):
        base = pl.multiple_of(i * tile, tile)
        limit = jnp.broadcast_to(reach[pl.ds(base, tile), :], (tile, HD))
        parts = out.shape[1] // HD

        def group(masked, a, accs):
            start = pl.multiple_of(base + TAPS - 8 * a, 8)
            tap_rows = taps[pl.ds(pl.multiple_of(8 * a, 8), 8), :]
            accs = list(accs)
            for r in range(8):
                keep = limit >= 8 * a + r if masked else None
                for p in range(parts):
                    lanes = slice(p * HD, (p + 1) * HD)
                    window = shifted[r, pl.ds(start, tile), lanes]
                    term = tap_rows[r : r + 1, lanes] * window
                    accs[p] = accs[p] + (jnp.where(keep, term, 0.0) if masked else term)
            return tuple(accs)

        zero = tuple(jnp.zeros((tile, HD), F32) for _ in range(parts))
        free = jnp.minimum(least[i] + 1, TAPS) // 8
        stop = jnp.minimum(most[i] // 8 + 1, TAPS // 8)
        accs = lax.fori_loop(0, free, functools.partial(group, False), zero)
        accs = lax.fori_loop(free, stop, functools.partial(group, True), accs)
        for p in range(parts):
            lanes = slice(p * HD, (p + 1) * HD)
            query = gate[pl.ds(base, tile), lanes].astype(F32)
            out[pl.ds(base, tile), lanes] = (query * accs[p]).astype(BF)
        return carry

    lax.fori_loop(0, rows // tile, row_tile, 0)


def filtered(extended, taps, reach, gate):
    rows, width = gate.shape
    tile = 64
    grouped = reach.reshape(rows // tile, tile)
    return pl.pallas_call(
        functools.partial(filter_kernel, tile),
        out_shape=jax.ShapeDtypeStruct((rows, width), BF),
        in_specs=[SMEM] * 2 + [VMEM] * 4,
        out_specs=VMEM,
        scratch_shapes=[pltpu.VMEM((8, rows + TAPS, width), F32)],
        compiler_params=pltpu.CompilerParams(vmem_limit_bytes=LIMIT),
        cost_estimate=pl.CostEstimate(
            flops=6 * TAPS * rows * width * 40, bytes_accessed=8 * rows * width, transcendentals=0
        ),
        name="filtered",
    )(jnp.min(grouped, axis=1), jnp.max(grouped, axis=1), extended, taps, reach, gate)


def attend_kernel(plan, first, last, me_ref, q_ref, begin_ref, *refs):
    refs = list(refs)
    pieces = [refs.pop(0) for _ in plan]
    before = [] if first else [refs.pop(0) for _ in range(3)]
    out = refs.pop(0) if last else None
    peak, total, running = refs
    me = me_ref[0]
    rows, width = q_ref.shape
    heads = width // HD
    chunk = 256
    scale = HD**-0.5 * math.log2(math.e)
    x = me % 4
    line = me // 4
    if first:
        peak[...] = jnp.full(peak.shape, NEG, F32)
        total[...] = jnp.zeros(total.shape, F32)
        running[...] = jnp.zeros(running.shape, F32)
    else:
        for now, then in zip((peak, total, running), before):
            now[...] = then[...]
    for piece, (dline, dx) in zip(pieces, plan):
        owner = (line - dline) * 4 + (x + dx) % 4

        @pl.when((line > 0) if dline else (owner <= me))
        def _(piece=piece, dline=dline, owner=owner):
            for base in range(0, rows, chunk):
                span = slice(base, base + chunk)
                begin = begin_ref[:, span]
                if dline:
                    open_row = begin <= owner * rows
                else:
                    key_at = owner * rows + lax.broadcasted_iota(jnp.int32, (rows, chunk), 0)
                    row_at = me * rows + base + lax.broadcasted_iota(jnp.int32, (1, chunk), 1)
                    allowed = (key_at <= row_at) & (key_at >= begin)
                for h in range(heads):
                    lanes = slice(h * HD, (h + 1) * HD)
                    keys = piece[:, lanes]
                    values = piece[:, width + h * HD : width + (h + 1) * HD]
                    scores = lax.dot_general(
                        keys, q_ref[span, lanes], (((1,), (1,)), ((), ())), preferred_element_type=F32
                    )
                    old = peak[h, :, span]
                    if dline:
                        top = jnp.max(scores, axis=0, keepdims=True)
                        new = jnp.where(open_row, jnp.maximum(old, top), old)
                        level = jnp.where(open_row, new, -NEG)
                    else:
                        scores = jnp.where(allowed, scores, NEG)
                        new = jnp.maximum(old, jnp.max(scores, axis=0, keepdims=True))
                        level = new
                    weights = jnp.exp2((scores - level) * scale)
                    factor = jnp.exp2((old - new) * scale)
                    peak[h, :, span] = new
                    total[h, :, span] = total[h, :, span] * factor + jnp.sum(weights, axis=0, keepdims=True)
                    update = lax.dot_general(
                        values, weights.astype(BF), (((0,), (0,)), ((), ())), preferred_element_type=F32
                    )
                    running[h, :, span] = running[h, :, span] * factor + update

    if last:
        for h in range(heads):
            out[:, h * HD : (h + 1) * HD] = (running[h] / total[h]).T.astype(BF)


def attend(me, queries, begins, plan, pieces, before=None, last=False):
    rows, width = queries.shape
    heads = width // HD
    state = [(heads, 1, rows), (heads, 1, rows), (heads, HD, rows)]
    if last:
        out_shape = jax.ShapeDtypeStruct((rows, width), BF)
        scratch = [pltpu.VMEM(s, F32) for s in state]
        out_specs = VMEM
    else:
        out_shape = tuple(jax.ShapeDtypeStruct(s, F32) for s in state)
        scratch = []
        out_specs = (VMEM,) * 3
    first = before is None
    before = () if first else tuple(before)
    return pl.pallas_call(
        functools.partial(attend_kernel, plan, first, last),
        out_shape=out_shape,
        in_specs=[SMEM] + [VMEM] * (2 + len(pieces) + len(before)),
        out_specs=out_specs,
        scratch_shapes=scratch,
        compiler_params=pltpu.CompilerParams(vmem_limit_bytes=LIMIT),
        cost_estimate=pl.CostEstimate(
            flops=4 * rows * rows * width * len(pieces) * 4,
            bytes_accessed=4 * (1 + len(pieces)) * rows * width,
            transcendentals=rows * rows * heads * len(pieces),
        ),
        name="attend",
    )(me, queries, begins, *pieces, *before)


def row_route(lines, pairs):
    return [(y * 4 + a, y * 4 + b) for y in lines for a, b in pairs]


ALL_UP = [(x, (x + 1) % 4) for x in range(4)]
ALL_DOWN = [(x, (x + 3) % 4) for x in range(4)]
ACROSS = [(x, 4 + x) for x in range(4)]


def attention(me, queries, begins, own):
    up = row_route((0,), ALL_UP) + row_route((1,), [(0, 1), (1, 2), (2, 3)])
    down = row_route((0,), ALL_DOWN) + row_route((1,), [(0, 3), (1, 0)])
    up_half = row_route((0,), ALL_UP) + row_route((1,), [(1, 2), (2, 3)])
    down_half = row_route((0,), ALL_DOWN) + row_route((1,), [(3, 2), (0, 3)])
    half = own.shape[0] // 2
    below = send(own, ACROSS, "seq")
    left = send(own, up, "seq")
    right = send(own, down, "seq")
    run = functools.partial(attend, me, queries, begins)
    state = run(((0, 0),), [own])
    below, left, right, state = lax.optimization_barrier((below, left, right, state))
    opposite = jnp.concatenate(
        [send(left[:half], up_half, "seq"), send(right[half:], down_half, "seq")], axis=0
    )
    far_left = send(below, row_route((1,), ALL_UP), "seq")
    far_right = send(below, row_route((1,), ALL_DOWN), "seq")
    state = run(((0, 3), (0, 1)), [left, right], state)
    opposite, state = lax.optimization_barrier((opposite, state))
    far_opposite = send(opposite, ACROSS, "seq")
    state = run(((0, 2), (1, 0)), [opposite, below], state)
    far_left, far_right, state = lax.optimization_barrier((far_left, far_right, state))
    state = run(((1, 3), (1, 1)), [far_left, far_right], state)
    far_opposite, state = lax.optimization_barrier((far_opposite, state))
    return run(((1, 2),), [far_opposite], state, True)


def segment_begin(positions, seg_starts):
    below = seg_starts[None, :] <= positions[:, None]
    return jnp.max(jnp.where(below, seg_starts[None, :], 0), axis=1)


def rotation_tables(positions):
    half_dim = HD // 2
    freqs = 10000.0 ** (-2.0 * jnp.arange(half_dim, dtype=F32) / HD)
    angles = positions.astype(F32)[:, None] * freqs[None, :]
    cosine = jnp.cos(angles)
    sine = jnp.sin(angles)
    return jnp.concatenate([cosine, cosine], axis=1), jnp.concatenate([-sine, sine], axis=1)


def shards(
    tokens,
    seg_starts,
    gain_hyena,
    w_hyena_in,
    hyena_filter,
    w_hyena_out,
    gain_attn,
    w_attn_in,
    w_attn_out,
):
    rows, width = tokens.shape
    me = lax.axis_index("seq").astype(jnp.int32)
    order = relative_order(lax.axis_index("tensor"))
    positions = me * rows + jnp.arange(rows, dtype=jnp.int32)
    begins = segment_begin(positions, seg_starts)
    reach = jnp.where(begins == 0, TAPS, positions - begins)[:, None]
    begins = begins[None, :]
    tables = rotation_tables(positions)

    def summed_over_tensor(values, weight):
        other = spread(values, weight, order[8:])
        return scatter_tensor(spread(values, weight, order[:8]), other)

    def stacked(weight):
        return weight.transpose(1, 0, 2)

    gain_hyena = gain_hyena.reshape(16, 1, width)
    gain_attn = gain_attn.reshape(16, 1, width)
    blocks = gather_tensor(with_squares(tokens.astype(F32)))
    product, gate = project((1, 2, 0), "hyena", blocks, order, gain_hyena, stacked(w_hyena_in))
    rim = send(product[rows - TAPS :], [(i, i + 1) for i in range(7)], "seq")
    tail = filtered(product, hyena_filter, reach[TAPS:], gate[TAPS:])
    head = filtered(
        jnp.concatenate([rim, product[:TAPS]], axis=0), hyena_filter, reach[:TAPS], gate[:TAPS]
    )
    gated = jnp.concatenate([head, tail], axis=0)
    middle = tokens.astype(F32) + summed_over_tensor(gated, w_hyena_out)
    blocks = gather_tensor(with_squares(middle))
    (own,) = project((1, 2), "attn", blocks, order, gain_attn, stacked(w_attn_in), tables)
    (queries,) = project((0,), "attn", blocks, order, gain_attn, stacked(w_attn_in), tables)
    context = attention(me[None], queries, begins, own)
    return middle + summed_over_tensor(context, w_attn_out)


def solution(mesh):
    placed = (
        P("seq", "tensor"),
        P(),
        P(),
        P(None, None, "tensor"),
        P(None, "tensor"),
        P("tensor", None),
        P(),
        P(None, None, "tensor"),
        P("tensor", None),
    )
    return jax.shard_map(
        shards, mesh=mesh, in_specs=placed, out_specs=P("seq", "tensor"), check_vma=False
    )
```

```python
import functools
import math

import jax
import jax.numpy as jnp
from jax import lax
from jax.experimental import pallas as pl
from jax.experimental.pallas import tpu as pltpu
from jax.sharding import PartitionSpec as P

HD = 128
TAPS = 128
BF = jnp.bfloat16
F32 = jnp.float32
NEG = -1e30
VMEM = pl.BlockSpec(memory_space=pltpu.VMEM)
SMEM = pl.BlockSpec(memory_space=pltpu.SMEM)
LIMIT = 10 * 2**20
EXTRA = 16
PROJECT_LIMIT = 46 * 2**20


def tensor_route(move):
    pairs = []
    for t in range(16):
        y, z, c = move(t // 8, t // 2 % 4, t % 2)
        pairs.append((t, (y % 2) * 8 + (z % 4) * 2 + c % 2))
    return pairs


ROUTE_Y = tensor_route(lambda y, z, c: (y + 1, z, c))
ROUTE_UP = tensor_route(lambda y, z, c: (y, z + 1, c))
ROUTE_DOWN = tensor_route(lambda y, z, c: (y, z - 1, c))
ROUTE_FAR = tensor_route(lambda y, z, c: (y, z + 2, c))
ROUTE_CORE = tensor_route(lambda y, z, c: (y, z, c + 1))


def send(block, route, axis="tensor"):
    return lax.ppermute(block, axis, route)


def gather_tensor(block):
    side = send(block, ROUTE_Y)
    below = send(block, ROUTE_UP)
    above = send(block, ROUTE_DOWN)
    far = send(block, ROUTE_FAR)
    side_below = send(side, ROUTE_UP)
    side_above = send(side, ROUTE_DOWN)
    side_far = send(far, ROUTE_Y)
    mine = [block, above, far, below, side, side_above, side_far, side_below]
    return mine + [send(one, ROUTE_CORE) for one in mine]


def with_squares(values):
    rows, width = values.shape
    square = jnp.sum(values * values, axis=1).reshape(rows // width, width)
    pieces = []
    for _ in range(3):
        piece = lax.reduce_precision(square, 8, 7)
        pieces.append(piece)
        square = square - piece
    pieces.append(jnp.zeros((EXTRA - 3 * (rows // width), width), F32))
    return jnp.concatenate([values, *pieces], axis=0).astype(BF)


def squares_kernel(values, out):
    rows, width = values.shape
    wide = values[...].astype(F32)
    out[0:rows, :] = values[...]
    total = jnp.sum((wide * wide).T, axis=0, keepdims=True)
    lines = []
    for _ in range(3):
        piece = total.astype(BF).astype(F32)
        total = total - piece
        lines += [piece[:, p : p + width] for p in range(0, rows, width)]
    lines.append(jnp.zeros((EXTRA - len(lines), width), F32))
    out[rows : rows + EXTRA, :] = jnp.concatenate(lines, axis=0).astype(BF)


def tokens_with_squares(tokens):
    rows, width = tokens.shape
    return pl.pallas_call(
        squares_kernel,
        out_shape=jax.ShapeDtypeStruct((rows + EXTRA, width), BF),
        in_specs=[VMEM],
        out_specs=VMEM,
        compiler_params=pltpu.CompilerParams(vmem_limit_bytes=LIMIT),
        cost_estimate=pl.CostEstimate(
            flops=3 * rows * width, bytes_accessed=4 * rows * width, transcendentals=0
        ),
        name="squares",
    )(tokens)


def relative_order(position):
    y, z, c = position // 8, position // 2 % 4, position % 2
    out = []
    for dc in range(2):
        for dy in range(2):
            for dz in range(4):
                out.append(((y + dy) % 2) * 8 + ((z + dz) % 4) * 2 + (c + dc) % 2)
    return jnp.stack(out).astype(jnp.int32)


def scatter_tensor(mine, other):
    received = send(other, ROUTE_CORE)

    def part(i):
        return (mine[i].astype(F32) + received[i].astype(F32)).astype(BF)

    side = send(part(6), ROUTE_Y)
    up = send(part(5), ROUTE_UP)
    down = send(part(7), ROUTE_DOWN)
    two = (mine[2].astype(F32) + received[2].astype(F32) + side.astype(F32)).astype(BF)
    across = mine[4].astype(F32) + received[4].astype(F32) + up.astype(F32) + down.astype(F32)
    above = send(part(1), ROUTE_UP)
    below = send(part(3), ROUTE_DOWN)
    two, across = lax.optimization_barrier((two, across.astype(BF)))
    back = send(across, ROUTE_Y)
    far = send(two, ROUTE_FAR)
    near = mine[0].astype(F32) + received[0].astype(F32) + above.astype(F32) + below.astype(F32)
    return near + far.astype(F32) + back.astype(F32)


def project_kernel(streams, kind, order, *refs):
    blocks, (gain, weight), refs = refs[:16], refs[16:18], refs[18:]
    if kind == "attn":
        cosine, sine = refs[:2]
        refs = refs[2:]
    outs, (scaled, held, sems) = refs[:-3], refs[-3:]
    copies = [
        pltpu.make_async_copy(
            weight.at[j], held.at[:, pl.ds(n * held.shape[1] // len(streams), held.shape[1] // len(streams))], sems.at[n]
        )
        for n, j in enumerate(streams)
    ]
    for copy in copies:
        copy.start()
    width = blocks[0].shape[1]
    rows = blocks[0].shape[0] - EXTRA
    parts = rows // width
    square = sum(block[rows : rows + EXTRA, :].astype(F32) for block in blocks)
    square = square[0:parts] + square[parts : 2 * parts] + square[2 * parts : 3 * parts]
    square = jnp.concatenate([square, jnp.zeros((8 - parts, width), F32)], axis=0)
    factor = lax.rsqrt(square / (16 * width) + 1e-05).T
    for k in range(16):
        columns = pl.ds(pl.multiple_of(order[k] * width, width), width)
        for p in range(parts):
            span = slice(p * width, (p + 1) * width)
            wide = blocks[k][span, :].astype(F32)
            scaled[span, columns] = (wide * factor[:, p : p + 1] * gain[order[k]]).astype(BF)
    for copy in copies:
        copy.wait()
    whole = jnp.dot(scaled[...], held[...], preferred_element_type=F32).astype(BF)
    halves = [whole[:, n * width : (n + 1) * width] for n in range(len(streams))]

    def rotated(half):
        done = []
        for h in range(width // HD):
            head = half[:, h * HD : (h + 1) * HD].astype(F32)
            turned = pltpu.roll(head, HD // 2, 1)
            done.append((head * cosine[...] + turned * sine[...]).astype(BF))
        return jnp.concatenate(done, axis=1)

    if kind == "hyena":
        outs[0][...] = (halves[0].astype(F32) * halves[1].astype(F32)).astype(BF)
        outs[1][...] = halves[2]
    elif len(streams) == 2:
        outs[0][:, 0:width] = rotated(halves[0])
        outs[0][:, width : 2 * width] = halves[1]
    else:
        outs[0][...] = rotated(halves[0])


def project(streams, kind, blocks, order, gain, weight, tables=()):
    rows, width = blocks[0].shape[0] - EXTRA, blocks[0].shape[1]
    features = 16 * width
    count = len(streams)
    if kind == "hyena":
        out_shape = tuple(jax.ShapeDtypeStruct((rows, width), BF) for _ in range(2))
    else:
        out_shape = (jax.ShapeDtypeStruct((rows, count * width), BF),)
    return pl.pallas_call(
        functools.partial(project_kernel, streams, kind),
        out_shape=out_shape,
        in_specs=[SMEM] + [VMEM] * 17 + [pl.BlockSpec(memory_space=pltpu.HBM)] + [VMEM] * len(tables),
        out_specs=(VMEM,) * len(out_shape),
        scratch_shapes=[
            pltpu.VMEM((rows, features), BF),
            pltpu.VMEM((features, count * width), BF),
            pltpu.SemaphoreType.DMA((count,)),
        ],
        compiler_params=pltpu.CompilerParams(vmem_limit_bytes=PROJECT_LIMIT),
        cost_estimate=pl.CostEstimate(
            flops=2 * rows * features * width * count,
            bytes_accessed=2 * features * (rows + count * width),
            transcendentals=0,
        ),
        name=f"project_{kind}",
    )(order, *blocks, gain, weight, *tables)


def spread_kernel(order, x, weight, out):
    wide = out.shape[2]
    for k in range(out.shape[0]):
        columns = pl.ds(pl.multiple_of(order[k] * wide, wide), wide)
        out[k] = jnp.dot(x[...], weight[:, columns], preferred_element_type=F32).astype(BF)


def spread(x, weight, order):
    rows, wide = x.shape
    count = order.shape[0]
    return pl.pallas_call(
        spread_kernel,
        out_shape=jax.ShapeDtypeStruct((count, rows, wide), BF),
        in_specs=[SMEM, VMEM, VMEM],
        out_specs=VMEM,
        compiler_params=pltpu.CompilerParams(vmem_limit_bytes=LIMIT),
        cost_estimate=pl.CostEstimate(
            flops=2 * rows * wide * wide * count,
            bytes_accessed=2 * (rows * wide + wide * wide * count + rows * wide * count),
            transcendentals=0,
        ),
        name="spread",
    )(order, x, weight)


def filter_kernel(tile, least, most, extended, taps, reach, gate, out, shifted):
    total = extended.shape[0]
    rows = out.shape[0]
    wide = extended[...].astype(F32)
    shifted[0] = wide
    for r in range(1, 8):
        shifted[r, 8:total] = shifted[0, 8 - r : total - r]

    def row_tile(i, carry):
        base = pl.multiple_of(i * tile, tile)
        limit = jnp.broadcast_to(reach[pl.ds(base, tile), :], (tile, HD))
        parts = out.shape[1] // HD

        def group(masked, a, accs):
            start = pl.multiple_of(base + TAPS - 8 * a, 8)
            tap_rows = taps[pl.ds(pl.multiple_of(8 * a, 8), 8), :]
            accs = list(accs)
            for r in range(8):
                keep = limit >= 8 * a + r if masked else None
                for p in range(parts):
                    lanes = slice(p * HD, (p + 1) * HD)
                    window = shifted[r, pl.ds(start, tile), lanes]
                    term = tap_rows[r : r + 1, lanes] * window
                    accs[p] = accs[p] + (jnp.where(keep, term, 0.0) if masked else term)
            return tuple(accs)

        zero = tuple(jnp.zeros((tile, HD), F32) for _ in range(parts))
        free = jnp.minimum(least[i] + 1, TAPS) // 8
        stop = jnp.minimum(most[i] // 8 + 1, TAPS // 8)
        accs = lax.fori_loop(0, free, functools.partial(group, False), zero)
        accs = lax.fori_loop(free, stop, functools.partial(group, True), accs)
        for p in range(parts):
            lanes = slice(p * HD, (p + 1) * HD)
            query = gate[pl.ds(base, tile), lanes].astype(F32)
            out[pl.ds(base, tile), lanes] = (query * accs[p]).astype(BF)
        return carry

    lax.fori_loop(0, rows // tile, row_tile, 0)


def filtered(extended, taps, reach, gate):
    rows, width = gate.shape
    tile = 64
    grouped = reach.reshape(rows // tile, tile)
    return pl.pallas_call(
        functools.partial(filter_kernel, tile),
        out_shape=jax.ShapeDtypeStruct((rows, width), BF),
        in_specs=[SMEM] * 2 + [VMEM] * 4,
        out_specs=VMEM,
        scratch_shapes=[pltpu.VMEM((8, rows + TAPS, width), F32)],
        compiler_params=pltpu.CompilerParams(vmem_limit_bytes=LIMIT),
        cost_estimate=pl.CostEstimate(
            flops=6 * TAPS * rows * width * 40, bytes_accessed=8 * rows * width, transcendentals=0
        ),
        name="filtered",
    )(jnp.min(grouped, axis=1), jnp.max(grouped, axis=1), extended, taps, reach, gate)


def attend_kernel(plan, first, last, me_ref, q_ref, begin_ref, *refs):
    refs = list(refs)
    pieces = [refs.pop(0) for _ in plan]
    before = [] if first else [refs.pop(0) for _ in range(3)]
    out = refs.pop(0) if last else None
    peak, total, running = refs
    me = me_ref[0]
    rows, width = q_ref.shape
    heads = width // HD
    chunk = 512
    scale = HD**-0.5 * math.log2(math.e)
    x = me % 4
    line = me // 4
    if first:
        peak[...] = jnp.full(peak.shape, NEG, F32)
        total[...] = jnp.zeros(total.shape, F32)
        running[...] = jnp.zeros(running.shape, F32)
    else:
        for now, then in zip((peak, total, running), before):
            now[...] = then[...]
    for piece, (dline, dx) in zip(pieces, plan):
        owner = (line - dline) * 4 + (x + dx) % 4

        @pl.when((line > 0) if dline else (owner <= me))
        def _(piece=piece, dline=dline, owner=owner):
            for base in range(0, rows, chunk):
                span = slice(base, base + chunk)
                begin = begin_ref[:, span]
                if dline:
                    open_row = begin <= owner * rows
                else:
                    key_at = owner * rows + lax.broadcasted_iota(jnp.int32, (rows, chunk), 0)
                    row_at = me * rows + base + lax.broadcasted_iota(jnp.int32, (1, chunk), 1)
                    allowed = (key_at <= row_at) & (key_at >= begin)
                for h in range(heads):
                    lanes = slice(h * HD, (h + 1) * HD)
                    keys = piece[:, lanes]
                    values = piece[:, width + h * HD : width + (h + 1) * HD]
                    scores = lax.dot_general(
                        keys, q_ref[span, lanes], (((1,), (1,)), ((), ())), preferred_element_type=F32
                    )
                    old = peak[h, :, span]
                    if dline:
                        top = jnp.max(scores, axis=0, keepdims=True)
                        new = jnp.where(open_row, jnp.maximum(old, top), old)
                        level = jnp.where(open_row, new, -NEG)
                    else:
                        scores = jnp.where(allowed, scores, NEG)
                        new = jnp.maximum(old, jnp.max(scores, axis=0, keepdims=True))
                        level = new
                    weights = jnp.exp2((scores - level) * scale)
                    factor = jnp.exp2((old - new) * scale)
                    peak[h, :, span] = new
                    total[h, :, span] = total[h, :, span] * factor + jnp.sum(weights, axis=0, keepdims=True)
                    update = lax.dot_general(
                        values, weights.astype(BF), (((0,), (0,)), ((), ())), preferred_element_type=F32
                    )
                    running[h, :, span] = running[h, :, span] * factor + update

    if last:
        for h in range(heads):
            out[:, h * HD : (h + 1) * HD] = (running[h] / total[h]).T.astype(BF)


def attend(me, queries, begins, plan, pieces, before=None, last=False):
    rows, width = queries.shape
    heads = width // HD
    state = [(heads, 1, rows), (heads, 1, rows), (heads, HD, rows)]
    if last:
        out_shape = jax.ShapeDtypeStruct((rows, width), BF)
        scratch = [pltpu.VMEM(s, F32) for s in state]
        out_specs = VMEM
    else:
        out_shape = tuple(jax.ShapeDtypeStruct(s, F32) for s in state)
        scratch = []
        out_specs = (VMEM,) * 3
    first = before is None
    before = () if first else tuple(before)
    return pl.pallas_call(
        functools.partial(attend_kernel, plan, first, last),
        out_shape=out_shape,
        in_specs=[SMEM] + [VMEM] * (2 + len(pieces) + len(before)),
        out_specs=out_specs,
        scratch_shapes=scratch,
        compiler_params=pltpu.CompilerParams(vmem_limit_bytes=LIMIT),
        cost_estimate=pl.CostEstimate(
            flops=4 * rows * rows * width * len(pieces) * 4,
            bytes_accessed=4 * (1 + len(pieces)) * rows * width,
            transcendentals=rows * rows * heads * len(pieces),
        ),
        name="attend",
    )(me, queries, begins, *pieces, *before)


def row_route(lines, pairs):
    return [(y * 4 + a, y * 4 + b) for y in lines for a, b in pairs]


ALL_UP = [(x, (x + 1) % 4) for x in range(4)]
ALL_DOWN = [(x, (x + 3) % 4) for x in range(4)]
ACROSS = [(x, 4 + x) for x in range(4)]


def attention(me, queries, begins, own):
    up = row_route((0,), ALL_UP) + row_route((1,), [(0, 1), (1, 2), (2, 3)])
    down = row_route((0,), ALL_DOWN) + row_route((1,), [(0, 3), (1, 0)])
    two_up = row_route((0,), [(x, (x + 2) % 4) for x in range(4)]) + row_route((1,), [(0, 2), (1, 3)])
    below = send(own, ACROSS, "seq")
    left = send(own, up, "seq")
    right = send(own, down, "seq")
    opposite = send(own, two_up, "seq")
    run = functools.partial(attend, me, queries, begins)
    state = run(((0, 0),), [own])
    below, state = lax.optimization_barrier((below, state))
    far_left = send(below, row_route((1,), ALL_UP), "seq")
    far_right = send(below, row_route((1,), ALL_DOWN), "seq")
    state = run(((0, 3), (0, 1)), [left, right], state)
    opposite, state = lax.optimization_barrier((opposite, state))
    far_opposite = send(opposite, ACROSS, "seq")
    state = run(((0, 2), (1, 0)), [opposite, below], state)
    far_left, far_right, state = lax.optimization_barrier((far_left, far_right, state))
    state = run(((1, 3), (1, 1)), [far_left, far_right], state)
    far_opposite, state = lax.optimization_barrier((far_opposite, state))
    return run(((1, 2),), [far_opposite], state, True)


def segment_begin(positions, seg_starts):
    below = seg_starts[None, :] <= positions[:, None]
    return jnp.max(jnp.where(below, seg_starts[None, :], 0), axis=1)


def rotation_tables(positions):
    half_dim = HD // 2
    freqs = 10000.0 ** (-2.0 * jnp.arange(half_dim, dtype=F32) / HD)
    angles = positions.astype(F32)[:, None] * freqs[None, :]
    cosine = jnp.cos(angles)
    sine = jnp.sin(angles)
    return jnp.concatenate([cosine, cosine], axis=1), jnp.concatenate([-sine, sine], axis=1)


def shards(
    tokens,
    seg_starts,
    gain_hyena,
    w_hyena_in,
    hyena_filter,
    w_hyena_out,
    gain_attn,
    w_attn_in,
    w_attn_out,
):
    rows, width = tokens.shape
    me = lax.axis_index("seq").astype(jnp.int32)
    order = relative_order(lax.axis_index("tensor"))
    positions = me * rows + jnp.arange(rows, dtype=jnp.int32)
    begins = segment_begin(positions, seg_starts)
    reach = jnp.where(begins == 0, TAPS, positions - begins)[:, None]
    begins = begins[None, :]
    tables = rotation_tables(positions)

    def summed_over_tensor(values, weight):
        other = spread(values, weight, order[8:])
        return scatter_tensor(spread(values, weight, order[:8]), other)

    def stacked(weight):
        return weight.transpose(1, 0, 2)

    gain_hyena = gain_hyena.reshape(16, 1, width)
    gain_attn = gain_attn.reshape(16, 1, width)
    blocks = gather_tensor(tokens_with_squares(tokens))
    product, gate = project((1, 2, 0), "hyena", blocks, order, gain_hyena, stacked(w_hyena_in))
    rim = send(product[rows - TAPS :], [(i, i + 1) for i in range(7)], "seq")
    tail = filtered(product, hyena_filter, reach[TAPS:], gate[TAPS:])
    head = filtered(
        jnp.concatenate([rim, product[:TAPS]], axis=0), hyena_filter, reach[:TAPS], gate[:TAPS]
    )
    gated = jnp.concatenate([head, tail], axis=0)
    middle = tokens.astype(F32) + summed_over_tensor(gated, w_hyena_out)
    blocks = gather_tensor(with_squares(middle))
    (own,) = project((1, 2), "attn", blocks, order, gain_attn, stacked(w_attn_in), tables)
    (queries,) = project((0,), "attn", blocks, order, gain_attn, stacked(w_attn_in), tables)
    context = attention(me[None], queries, begins, own)
    return middle + summed_over_tensor(context, w_attn_out)


def solution(mesh):
    placed = (
        P("seq", "tensor"),
        P(),
        P(),
        P(None, None, "tensor"),
        P(None, "tensor"),
        P("tensor", None),
        P(),
        P(None, None, "tensor"),
        P("tensor", None),
    )
    return jax.shard_map(
        shards, mesh=mesh, in_specs=placed, out_specs=P("seq", "tensor"), check_vma=False
    )
```

```python
import functools
import math

import jax
import jax.numpy as jnp
from jax import lax
from jax.experimental import pallas as pl
from jax.experimental.pallas import tpu as pltpu
from jax.sharding import PartitionSpec as P

HD = 128
TAPS = 128
BF = jnp.bfloat16
F32 = jnp.float32
NEG = -1e30
VMEM = pl.BlockSpec(memory_space=pltpu.VMEM)
SMEM = pl.BlockSpec(memory_space=pltpu.SMEM)
LIMIT = 10 * 2**20
EXTRA = 16
PROJECT_LIMIT = 46 * 2**20


def tensor_route(move):
    pairs = []
    for t in range(16):
        y, z, c = move(t // 8, t // 2 % 4, t % 2)
        pairs.append((t, (y % 2) * 8 + (z % 4) * 2 + c % 2))
    return pairs


ROUTE_Y = tensor_route(lambda y, z, c: (y + 1, z, c))
ROUTE_UP = tensor_route(lambda y, z, c: (y, z + 1, c))
ROUTE_DOWN = tensor_route(lambda y, z, c: (y, z - 1, c))
ROUTE_FAR = tensor_route(lambda y, z, c: (y, z + 2, c))
ROUTE_CORE = tensor_route(lambda y, z, c: (y, z, c + 1))


def send(block, route, axis="tensor"):
    return lax.ppermute(block, axis, route)


def gather_tensor(block):
    side = send(block, ROUTE_Y)
    below = send(block, ROUTE_UP)
    above = send(block, ROUTE_DOWN)
    far = send(block, ROUTE_FAR)
    side_below = send(side, ROUTE_UP)
    side_above = send(side, ROUTE_DOWN)
    side_far = send(far, ROUTE_Y)
    mine = [block, above, far, below, side, side_above, side_far, side_below]
    return mine + [send(one, ROUTE_CORE) for one in mine]


def with_squares(values):
    rows, width = values.shape
    square = jnp.sum(values * values, axis=1).reshape(rows // width, width)
    pieces = []
    for _ in range(3):
        piece = lax.reduce_precision(square, 8, 7)
        pieces.append(piece)
        square = square - piece
    pieces.append(jnp.zeros((EXTRA - 3 * (rows // width), width), F32))
    return jnp.concatenate([values, *pieces], axis=0).astype(BF)


def squares_kernel(values, out):
    rows, width = values.shape
    wide = values[...].astype(F32)
    out[0:rows, :] = values[...]
    total = jnp.sum((wide * wide).T, axis=0, keepdims=True)
    lines = []
    for _ in range(3):
        piece = total.astype(BF).astype(F32)
        total = total - piece
        lines += [piece[:, p : p + width] for p in range(0, rows, width)]
    lines.append(jnp.zeros((EXTRA - len(lines), width), F32))
    out[rows : rows + EXTRA, :] = jnp.concatenate(lines, axis=0).astype(BF)


def tokens_with_squares(tokens):
    rows, width = tokens.shape
    return pl.pallas_call(
        squares_kernel,
        out_shape=jax.ShapeDtypeStruct((rows + EXTRA, width), BF),
        in_specs=[VMEM],
        out_specs=VMEM,
        compiler_params=pltpu.CompilerParams(vmem_limit_bytes=LIMIT),
        cost_estimate=pl.CostEstimate(
            flops=3 * rows * width, bytes_accessed=4 * rows * width, transcendentals=0
        ),
        name="squares",
    )(tokens)


def relative_order(position):
    y, z, c = position // 8, position // 2 % 4, position % 2
    out = []
    for dc in range(2):
        for dy in range(2):
            for dz in range(4):
                out.append(((y + dy) % 2) * 8 + ((z + dz) % 4) * 2 + (c + dc) % 2)
    return jnp.stack(out).astype(jnp.int32)


SOON = (6, 5, 7, 1, 3)
LATER = (2, 4, 0)


def scatter_tensor(mine, soon, later):
    soon = send(soon, ROUTE_CORE)
    later = send(later, ROUTE_CORE)
    received = {i: soon[n] for n, i in enumerate(SOON)}
    received.update({i: later[n] for n, i in enumerate(LATER)})

    def part(i):
        return (mine[i].astype(F32) + received[i].astype(F32)).astype(BF)

    side = send(part(6), ROUTE_Y)
    up = send(part(5), ROUTE_UP)
    down = send(part(7), ROUTE_DOWN)
    two = (mine[2].astype(F32) + received[2].astype(F32) + side.astype(F32)).astype(BF)
    across = mine[4].astype(F32) + received[4].astype(F32) + up.astype(F32) + down.astype(F32)
    above = send(part(1), ROUTE_UP)
    below = send(part(3), ROUTE_DOWN)
    two, across = lax.optimization_barrier((two, across.astype(BF)))
    back = send(across, ROUTE_Y)
    far = send(two, ROUTE_FAR)
    near = mine[0].astype(F32) + received[0].astype(F32) + above.astype(F32) + below.astype(F32)
    return near + far.astype(F32) + back.astype(F32)


def project_kernel(streams, kind, order, *refs):
    blocks, (gain, weight), refs = refs[:16], refs[16:18], refs[18:]
    if kind == "attn":
        cosine, sine = refs[:2]
        refs = refs[2:]
    outs, (scaled, held, sems) = refs[:-3], refs[-3:]
    copies = [
        pltpu.make_async_copy(
            weight.at[j], held.at[:, pl.ds(n * held.shape[1] // len(streams), held.shape[1] // len(streams))], sems.at[n]
        )
        for n, j in enumerate(streams)
    ]
    for copy in copies:
        copy.start()
    width = blocks[0].shape[1]
    rows = blocks[0].shape[0] - EXTRA
    parts = rows // width
    square = sum(block[rows : rows + EXTRA, :].astype(F32) for block in blocks)
    square = square[0:parts] + square[parts : 2 * parts] + square[2 * parts : 3 * parts]
    square = jnp.concatenate([square, jnp.zeros((8 - parts, width), F32)], axis=0)
    factor = lax.rsqrt(square / (16 * width) + 1e-05).T
    for k in range(16):
        columns = pl.ds(pl.multiple_of(order[k] * width, width), width)
        for p in range(parts):
            span = slice(p * width, (p + 1) * width)
            wide = blocks[k][span, :].astype(F32)
            scaled[span, columns] = (wide * factor[:, p : p + 1] * gain[order[k]]).astype(BF)
    for copy in copies:
        copy.wait()
    whole = jnp.dot(scaled[...], held[...], preferred_element_type=F32).astype(BF)
    halves = [whole[:, n * width : (n + 1) * width] for n in range(len(streams))]

    def rotated(half):
        done = []
        for h in range(width // HD):
            head = half[:, h * HD : (h + 1) * HD].astype(F32)
            turned = pltpu.roll(head, HD // 2, 1)
            done.append((head * cosine[...] + turned * sine[...]).astype(BF))
        return jnp.concatenate(done, axis=1)

    if kind == "hyena":
        outs[0][...] = (halves[0].astype(F32) * halves[1].astype(F32)).astype(BF)
        outs[1][...] = halves[2]
    elif len(streams) == 2:
        outs[0][:, 0:width] = rotated(halves[0])
        outs[0][:, width : 2 * width] = halves[1]
    else:
        outs[0][...] = rotated(halves[0])


def project(streams, kind, blocks, order, gain, weight, tables=()):
    rows, width = blocks[0].shape[0] - EXTRA, blocks[0].shape[1]
    features = 16 * width
    count = len(streams)
    if kind == "hyena":
        out_shape = tuple(jax.ShapeDtypeStruct((rows, width), BF) for _ in range(2))
    else:
        out_shape = (jax.ShapeDtypeStruct((rows, count * width), BF),)
    return pl.pallas_call(
        functools.partial(project_kernel, streams, kind),
        out_shape=out_shape,
        in_specs=[SMEM] + [VMEM] * 17 + [pl.BlockSpec(memory_space=pltpu.HBM)] + [VMEM] * len(tables),
        out_specs=(VMEM,) * len(out_shape),
        scratch_shapes=[
            pltpu.VMEM((rows, features), BF),
            pltpu.VMEM((features, count * width), BF),
            pltpu.SemaphoreType.DMA((count,)),
        ],
        compiler_params=pltpu.CompilerParams(vmem_limit_bytes=PROJECT_LIMIT),
        cost_estimate=pl.CostEstimate(
            flops=2 * rows * features * width * count,
            bytes_accessed=2 * features * (rows + count * width),
            transcendentals=0,
        ),
        name=f"project_{kind}",
    )(order, *blocks, gain, weight, *tables)


def spread_kernel(order, x, weight, out):
    wide = out.shape[2]
    for k in range(out.shape[0]):
        columns = pl.ds(pl.multiple_of(order[k] * wide, wide), wide)
        out[k] = jnp.dot(x[...], weight[:, columns], preferred_element_type=F32).astype(BF)


def spread(x, weight, order):
    rows, wide = x.shape
    count = order.shape[0]
    return pl.pallas_call(
        spread_kernel,
        out_shape=jax.ShapeDtypeStruct((count, rows, wide), BF),
        in_specs=[SMEM, VMEM, VMEM],
        out_specs=VMEM,
        compiler_params=pltpu.CompilerParams(vmem_limit_bytes=LIMIT),
        cost_estimate=pl.CostEstimate(
            flops=2 * rows * wide * wide * count,
            bytes_accessed=2 * (rows * wide + wide * wide * count + rows * wide * count),
            transcendentals=0,
        ),
        name="spread",
    )(order, x, weight)


def filter_kernel(tile, least, most, extended, taps, reach, gate, out, shifted):
    total = extended.shape[0]
    rows = out.shape[0]
    wide = extended[...].astype(F32)
    shifted[0] = wide
    for r in range(1, 8):
        shifted[r, 8:total] = shifted[0, 8 - r : total - r]

    def row_tile(i, carry):
        base = pl.multiple_of(i * tile, tile)
        limit = jnp.broadcast_to(reach[pl.ds(base, tile), :], (tile, HD))
        parts = out.shape[1] // HD

        def group(masked, a, accs):
            start = pl.multiple_of(base + TAPS - 8 * a, 8)
            tap_rows = taps[pl.ds(pl.multiple_of(8 * a, 8), 8), :]
            accs = list(accs)
            for r in range(8):
                keep = limit >= 8 * a + r if masked else None
                for p in range(parts):
                    lanes = slice(p * HD, (p + 1) * HD)
                    window = shifted[r, pl.ds(start, tile), lanes]
                    term = tap_rows[r : r + 1, lanes] * window
                    accs[p] = accs[p] + (jnp.where(keep, term, 0.0) if masked else term)
            return tuple(accs)

        zero = tuple(jnp.zeros((tile, HD), F32) for _ in range(parts))
        free = jnp.minimum(least[i] + 1, TAPS) // 8
        stop = jnp.minimum(most[i] // 8 + 1, TAPS // 8)
        accs = lax.fori_loop(0, free, functools.partial(group, False), zero)
        accs = lax.fori_loop(free, stop, functools.partial(group, True), accs)
        for p in range(parts):
            lanes = slice(p * HD, (p + 1) * HD)
            query = gate[pl.ds(base, tile), lanes].astype(F32)
            out[pl.ds(base, tile), lanes] = (query * accs[p]).astype(BF)
        return carry

    lax.fori_loop(0, rows // tile, row_tile, 0)


def filtered(extended, taps, reach, gate):
    rows, width = gate.shape
    tile = 64
    grouped = reach.reshape(rows // tile, tile)
    return pl.pallas_call(
        functools.partial(filter_kernel, tile),
        out_shape=jax.ShapeDtypeStruct((rows, width), BF),
        in_specs=[SMEM] * 2 + [VMEM] * 4,
        out_specs=VMEM,
        scratch_shapes=[pltpu.VMEM((8, rows + TAPS, width), F32)],
        compiler_params=pltpu.CompilerParams(vmem_limit_bytes=LIMIT),
        cost_estimate=pl.CostEstimate(
            flops=6 * TAPS * rows * width * 40, bytes_accessed=8 * rows * width, transcendentals=0
        ),
        name="filtered",
    )(jnp.min(grouped, axis=1), jnp.max(grouped, axis=1), extended, taps, reach, gate)


def attend_kernel(plan, first, last, me_ref, q_ref, begin_ref, *refs):
    refs = list(refs)
    pieces = [refs.pop(0) for _ in plan]
    before = [] if first else [refs.pop(0) for _ in range(3)]
    out = refs.pop(0) if last else None
    peak, total, running = refs
    me = me_ref[0]
    rows, width = q_ref.shape
    heads = width // HD
    chunk = 512
    scale = HD**-0.5 * math.log2(math.e)
    x = me % 4
    line = me // 4
    if first:
        peak[...] = jnp.full(peak.shape, NEG, F32)
        total[...] = jnp.zeros(total.shape, F32)
        running[...] = jnp.zeros(running.shape, F32)
    else:
        for now, then in zip((peak, total, running), before):
            now[...] = then[...]
    for piece, (dline, dx) in zip(pieces, plan):
        owner = (line - dline) * 4 + (x + dx) % 4

        @pl.when((line > 0) if dline else (owner <= me))
        def _(piece=piece, dline=dline, owner=owner):
            for base in range(0, rows, chunk):
                span = slice(base, base + chunk)
                begin = begin_ref[:, span]
                if dline:
                    open_row = begin <= owner * rows
                else:
                    key_at = owner * rows + lax.broadcasted_iota(jnp.int32, (rows, chunk), 0)
                    row_at = me * rows + base + lax.broadcasted_iota(jnp.int32, (1, chunk), 1)
                    allowed = (key_at <= row_at) & (key_at >= begin)
                for h in range(heads):
                    lanes = slice(h * HD, (h + 1) * HD)
                    keys = piece[:, lanes]
                    values = piece[:, width + h * HD : width + (h + 1) * HD]
                    scores = lax.dot_general(
                        keys, q_ref[span, lanes], (((1,), (1,)), ((), ())), preferred_element_type=F32
                    )
                    old = peak[h, :, span]
                    if dline:
                        top = jnp.max(scores, axis=0, keepdims=True)
                        new = jnp.where(open_row, jnp.maximum(old, top), old)
                        level = jnp.where(open_row, new, -NEG)
                    else:
                        scores = jnp.where(allowed, scores, NEG)
                        new = jnp.maximum(old, jnp.max(scores, axis=0, keepdims=True))
                        level = new
                    weights = jnp.exp2((scores - level) * scale)
                    factor = jnp.exp2((old - new) * scale)
                    peak[h, :, span] = new
                    total[h, :, span] = total[h, :, span] * factor + jnp.sum(weights, axis=0, keepdims=True)
                    update = lax.dot_general(
                        values, weights.astype(BF), (((0,), (0,)), ((), ())), preferred_element_type=F32
                    )
                    running[h, :, span] = running[h, :, span] * factor + update

    if last:
        for h in range(heads):
            out[:, h * HD : (h + 1) * HD] = (running[h] / total[h]).T.astype(BF)


def attend(me, queries, begins, plan, pieces, before=None, last=False):
    rows, width = queries.shape
    heads = width // HD
    state = [(heads, 1, rows), (heads, 1, rows), (heads, HD, rows)]
    if last:
        out_shape = jax.ShapeDtypeStruct((rows, width), BF)
        scratch = [pltpu.VMEM(s, F32) for s in state]
        out_specs = VMEM
    else:
        out_shape = tuple(jax.ShapeDtypeStruct(s, F32) for s in state)
        scratch = []
        out_specs = (VMEM,) * 3
    first = before is None
    before = () if first else tuple(before)
    return pl.pallas_call(
        functools.partial(attend_kernel, plan, first, last),
        out_shape=out_shape,
        in_specs=[SMEM] + [VMEM] * (2 + len(pieces) + len(before)),
        out_specs=out_specs,
        scratch_shapes=scratch,
        compiler_params=pltpu.CompilerParams(vmem_limit_bytes=LIMIT),
        cost_estimate=pl.CostEstimate(
            flops=4 * rows * rows * width * len(pieces) * 4,
            bytes_accessed=4 * (1 + len(pieces)) * rows * width,
            transcendentals=rows * rows * heads * len(pieces),
        ),
        name="attend",
    )(me, queries, begins, *pieces, *before)


def row_route(lines, pairs):
    return [(y * 4 + a, y * 4 + b) for y in lines for a, b in pairs]


ALL_UP = [(x, (x + 1) % 4) for x in range(4)]
ALL_DOWN = [(x, (x + 3) % 4) for x in range(4)]
ACROSS = [(x, 4 + x) for x in range(4)]


def attention(me, queries, begins, own):
    up = row_route((0,), ALL_UP) + row_route((1,), [(0, 1), (1, 2), (2, 3)])
    down = row_route((0,), ALL_DOWN) + row_route((1,), [(0, 3), (1, 0)])
    two_up = row_route((0,), [(x, (x + 2) % 4) for x in range(4)]) + row_route((1,), [(0, 2), (1, 3)])
    below = send(own, ACROSS, "seq")
    left = send(own, up, "seq")
    right = send(own, down, "seq")
    opposite = send(own, two_up, "seq")
    run = functools.partial(attend, me, queries, begins)
    state = run(((0, 0),), [own])
    below, state = lax.optimization_barrier((below, state))
    far_left = send(below, row_route((1,), ALL_UP), "seq")
    far_right = send(below, row_route((1,), ALL_DOWN), "seq")
    state = run(((0, 3), (0, 1)), [left, right], state)
    opposite, state = lax.optimization_barrier((opposite, state))
    far_opposite = send(opposite, ACROSS, "seq")
    state = run(((0, 2), (1, 0)), [opposite, below], state)
    far_left, far_right, state = lax.optimization_barrier((far_left, far_right, state))
    state = run(((1, 3), (1, 1)), [far_left, far_right], state)
    far_opposite, state = lax.optimization_barrier((far_opposite, state))
    return run(((1, 2),), [far_opposite], state, True)


def segment_begin(positions, seg_starts):
    below = seg_starts[None, :] <= positions[:, None]
    return jnp.max(jnp.where(below, seg_starts[None, :], 0), axis=1)


def rotation_tables(positions):
    half_dim = HD // 2
    freqs = 10000.0 ** (-2.0 * jnp.arange(half_dim, dtype=F32) / HD)
    angles = positions.astype(F32)[:, None] * freqs[None, :]
    cosine = jnp.cos(angles)
    sine = jnp.sin(angles)
    return jnp.concatenate([cosine, cosine], axis=1), jnp.concatenate([-sine, sine], axis=1)


def shards(
    tokens,
    seg_starts,
    gain_hyena,
    w_hyena_in,
    hyena_filter,
    w_hyena_out,
    gain_attn,
    w_attn_in,
    w_attn_out,
):
    rows, width = tokens.shape
    me = lax.axis_index("seq").astype(jnp.int32)
    order = relative_order(lax.axis_index("tensor"))
    positions = me * rows + jnp.arange(rows, dtype=jnp.int32)
    begins = segment_begin(positions, seg_starts)
    reach = jnp.where(begins == 0, TAPS, positions - begins)[:, None]
    begins = begins[None, :]
    tables = rotation_tables(positions)

    def summed_over_tensor(values, weight):
        soon, later = (
            spread(values, weight, jnp.stack([order[8 + i] for i in picks])) for picks in (SOON, LATER)
        )
        return scatter_tensor(spread(values, weight, order[:8]), soon, later)

    def stacked(weight):
        return weight.transpose(1, 0, 2)

    gain_hyena = gain_hyena.reshape(16, 1, width)
    gain_attn = gain_attn.reshape(16, 1, width)
    blocks = gather_tensor(tokens_with_squares(tokens))
    product, gate = project((1, 2, 0), "hyena", blocks, order, gain_hyena, stacked(w_hyena_in))
    rim = send(product[rows - TAPS :], [(i, i + 1) for i in range(7)], "seq")
    tail = filtered(product, hyena_filter, reach[TAPS:], gate[TAPS:])
    head = filtered(
        jnp.concatenate([rim, product[:TAPS]], axis=0), hyena_filter, reach[:TAPS], gate[:TAPS]
    )
    gated = jnp.concatenate([head, tail], axis=0)
    middle = tokens.astype(F32) + summed_over_tensor(gated, w_hyena_out)
    blocks = gather_tensor(with_squares(middle))
    (own,) = project((1, 2), "attn", blocks, order, gain_attn, stacked(w_attn_in), tables)
    (queries,) = project((0,), "attn", blocks, order, gain_attn, stacked(w_attn_in), tables)
    context = attention(me[None], queries, begins, own)
    return middle + summed_over_tensor(context, w_attn_out)


def solution(mesh):
    placed = (
        P("seq", "tensor"),
        P(),
        P(),
        P(None, None, "tensor"),
        P(None, "tensor"),
        P("tensor", None),
        P(),
        P(None, None, "tensor"),
        P("tensor", None),
    )
    return jax.shard_map(
        shards, mesh=mesh, in_specs=placed, out_specs=P("seq", "tensor"), check_vma=False
    )
```

```python
import functools
import math

import jax
import jax.numpy as jnp
from jax import lax
from jax.experimental import pallas as pl
from jax.experimental.pallas import tpu as pltpu
from jax.sharding import PartitionSpec as P

HD = 128
TAPS = 128
BF = jnp.bfloat16
F32 = jnp.float32
NEG = -1e30
VMEM = pl.BlockSpec(memory_space=pltpu.VMEM)
SMEM = pl.BlockSpec(memory_space=pltpu.SMEM)
LIMIT = 10 * 2**20
EXTRA = 16
PROJECT_LIMIT = 46 * 2**20


def tensor_route(move):
    pairs = []
    for t in range(16):
        y, z, c = move(t // 8, t // 2 % 4, t % 2)
        pairs.append((t, (y % 2) * 8 + (z % 4) * 2 + c % 2))
    return pairs


ROUTE_Y = tensor_route(lambda y, z, c: (y + 1, z, c))
ROUTE_UP = tensor_route(lambda y, z, c: (y, z + 1, c))
ROUTE_DOWN = tensor_route(lambda y, z, c: (y, z - 1, c))
ROUTE_FAR = tensor_route(lambda y, z, c: (y, z + 2, c))
ROUTE_CORE = tensor_route(lambda y, z, c: (y, z, c + 1))


def send(block, route, axis="tensor"):
    return lax.ppermute(block, axis, route)


def gather_tensor(block):
    side = send(block, ROUTE_Y)
    below = send(block, ROUTE_UP)
    above = send(block, ROUTE_DOWN)
    far = send(block, ROUTE_FAR)
    side_below = send(side, ROUTE_UP)
    side_above = send(side, ROUTE_DOWN)
    side_other = send(side, ROUTE_CORE)
    far, side_other = lax.optimization_barrier((far, side_other))
    side_far = send(far, ROUTE_Y)
    mine = [block, above, far, below, side, side_above, side_far, side_below]
    return mine + [side_other if one is side else send(one, ROUTE_CORE) for one in mine]


def with_squares(values):
    rows, width = values.shape
    square = jnp.sum(values * values, axis=1).reshape(rows // width, width)
    pieces = []
    for _ in range(3):
        piece = lax.reduce_precision(square, 8, 7)
        pieces.append(piece)
        square = square - piece
    pieces.append(jnp.zeros((EXTRA - 3 * (rows // width), width), F32))
    return jnp.concatenate([values, *pieces], axis=0).astype(BF)


def squares_kernel(values, out):
    rows, width = values.shape
    wide = values[...].astype(F32)
    out[0:rows, :] = values[...]
    total = jnp.sum((wide * wide).T, axis=0, keepdims=True)
    lines = []
    for _ in range(3):
        piece = total.astype(BF).astype(F32)
        total = total - piece
        lines += [piece[:, p : p + width] for p in range(0, rows, width)]
    lines.append(jnp.zeros((EXTRA - len(lines), width), F32))
    out[rows : rows + EXTRA, :] = jnp.concatenate(lines, axis=0).astype(BF)


def tokens_with_squares(tokens):
    rows, width = tokens.shape
    return pl.pallas_call(
        squares_kernel,
        out_shape=jax.ShapeDtypeStruct((rows + EXTRA, width), BF),
        in_specs=[VMEM],
        out_specs=VMEM,
        compiler_params=pltpu.CompilerParams(vmem_limit_bytes=LIMIT),
        cost_estimate=pl.CostEstimate(
            flops=3 * rows * width, bytes_accessed=4 * rows * width, transcendentals=0
        ),
        name="squares",
    )(tokens)


def relative_order(position):
    y, z, c = position // 8, position // 2 % 4, position % 2
    out = []
    for dc in range(2):
        for dy in range(2):
            for dz in range(4):
                out.append(((y + dy) % 2) * 8 + ((z + dz) % 4) * 2 + (c + dc) % 2)
    return jnp.stack(out).astype(jnp.int32)


def scatter_tensor(mine, other):
    received = send(other, ROUTE_CORE)

    def part(i):
        return (mine[i].astype(F32) + received[i].astype(F32)).astype(BF)

    side = send(part(6), ROUTE_Y)
    up = send(part(5), ROUTE_UP)
    down = send(part(7), ROUTE_DOWN)
    two = (mine[2].astype(F32) + received[2].astype(F32) + side.astype(F32)).astype(BF)
    across = mine[4].astype(F32) + received[4].astype(F32) + up.astype(F32) + down.astype(F32)
    above = send(part(1), ROUTE_UP)
    below = send(part(3), ROUTE_DOWN)
    two, across = lax.optimization_barrier((two, across.astype(BF)))
    back = send(across, ROUTE_Y)
    far = send(two, ROUTE_FAR)
    near = mine[0].astype(F32) + received[0].astype(F32) + above.astype(F32) + below.astype(F32)
    return near + far.astype(F32) + back.astype(F32)


def project_kernel(streams, kind, order, *refs):
    blocks, (gain, weight), refs = refs[:16], refs[16:18], refs[18:]
    if kind == "attn":
        cosine, sine = refs[:2]
        refs = refs[2:]
    outs, (scaled, held, sems) = refs[:-3], refs[-3:]
    copies = [
        pltpu.make_async_copy(
            weight.at[j], held.at[:, pl.ds(n * held.shape[1] // len(streams), held.shape[1] // len(streams))], sems.at[n]
        )
        for n, j in enumerate(streams)
    ]
    for copy in copies:
        copy.start()
    width = blocks[0].shape[1]
    rows = blocks[0].shape[0] - EXTRA
    parts = rows // width
    square = sum(block[rows : rows + EXTRA, :].astype(F32) for block in blocks)
    square = square[0:parts] + square[parts : 2 * parts] + square[2 * parts : 3 * parts]
    square = jnp.concatenate([square, jnp.zeros((8 - parts, width), F32)], axis=0)
    factor = lax.rsqrt(square / (16 * width) + 1e-05).T
    for k in range(16):
        columns = pl.ds(pl.multiple_of(order[k] * width, width), width)
        for p in range(parts):
            span = slice(p * width, (p + 1) * width)
            wide = blocks[k][span, :].astype(F32)
            scaled[span, columns] = (wide * factor[:, p : p + 1] * gain[order[k]]).astype(BF)
    for copy in copies:
        copy.wait()
    whole = jnp.dot(scaled[...], held[...], preferred_element_type=F32).astype(BF)
    halves = [whole[:, n * width : (n + 1) * width] for n in range(len(streams))]

    def rotated(half):
        done = []
        for h in range(width // HD):
            head = half[:, h * HD : (h + 1) * HD].astype(F32)
            turned = pltpu.roll(head, HD // 2, 1)
            done.append((head * cosine[...] + turned * sine[...]).astype(BF))
        return jnp.concatenate(done, axis=1)

    if kind == "hyena":
        outs[0][...] = (halves[0].astype(F32) * halves[1].astype(F32)).astype(BF)
        outs[1][...] = halves[2]
    elif len(streams) == 2:
        outs[0][:, 0:width] = rotated(halves[0])
        outs[0][:, width : 2 * width] = halves[1]
    else:
        outs[0][...] = rotated(halves[0])


def project(streams, kind, blocks, order, gain, weight, tables=()):
    rows, width = blocks[0].shape[0] - EXTRA, blocks[0].shape[1]
    features = 16 * width
    count = len(streams)
    if kind == "hyena":
        out_shape = tuple(jax.ShapeDtypeStruct((rows, width), BF) for _ in range(2))
    else:
        out_shape = (jax.ShapeDtypeStruct((rows, count * width), BF),)
    return pl.pallas_call(
        functools.partial(project_kernel, streams, kind),
        out_shape=out_shape,
        in_specs=[SMEM] + [VMEM] * 17 + [pl.BlockSpec(memory_space=pltpu.HBM)] + [VMEM] * len(tables),
        out_specs=(VMEM,) * len(out_shape),
        scratch_shapes=[
            pltpu.VMEM((rows, features), BF),
            pltpu.VMEM((features, count * width), BF),
            pltpu.SemaphoreType.DMA((count,)),
        ],
        compiler_params=pltpu.CompilerParams(vmem_limit_bytes=PROJECT_LIMIT),
        cost_estimate=pl.CostEstimate(
            flops=2 * rows * features * width * count,
            bytes_accessed=2 * features * (rows + count * width),
            transcendentals=0,
        ),
        name=f"project_{kind}",
    )(order, *blocks, gain, weight, *tables)


def spread_kernel(order, x, weight, out):
    wide = out.shape[2]
    for k in range(out.shape[0]):
        columns = pl.ds(pl.multiple_of(order[k] * wide, wide), wide)
        out[k] = jnp.dot(x[...], weight[:, columns], preferred_element_type=F32).astype(BF)


def spread(x, weight, order):
    rows, wide = x.shape
    count = order.shape[0]
    return pl.pallas_call(
        spread_kernel,
        out_shape=jax.ShapeDtypeStruct((count, rows, wide), BF),
        in_specs=[SMEM, VMEM, VMEM],
        out_specs=VMEM,
        compiler_params=pltpu.CompilerParams(vmem_limit_bytes=LIMIT),
        cost_estimate=pl.CostEstimate(
            flops=2 * rows * wide * wide * count,
            bytes_accessed=2 * (rows * wide + wide * wide * count + rows * wide * count),
            transcendentals=0,
        ),
        name="spread",
    )(order, x, weight)


def filter_kernel(tile, least, most, extended, taps, reach, gate, out, shifted):
    total = extended.shape[0]
    rows = out.shape[0]
    wide = extended[...].astype(F32)
    shifted[0] = wide
    for r in range(1, 8):
        shifted[r, 8:total] = shifted[0, 8 - r : total - r]

    def row_tile(i, carry):
        base = pl.multiple_of(i * tile, tile)
        limit = jnp.broadcast_to(reach[pl.ds(base, tile), :], (tile, HD))
        parts = out.shape[1] // HD

        def group(masked, a, accs):
            start = pl.multiple_of(base + TAPS - 8 * a, 8)
            tap_rows = taps[pl.ds(pl.multiple_of(8 * a, 8), 8), :]
            accs = list(accs)
            for r in range(8):
                keep = limit >= 8 * a + r if masked else None
                for p in range(parts):
                    lanes = slice(p * HD, (p + 1) * HD)
                    window = shifted[r, pl.ds(start, tile), lanes]
                    term = tap_rows[r : r + 1, lanes] * window
                    accs[p] = accs[p] + (jnp.where(keep, term, 0.0) if masked else term)
            return tuple(accs)

        zero = tuple(jnp.zeros((tile, HD), F32) for _ in range(parts))
        free = jnp.minimum(least[i] + 1, TAPS) // 8
        stop = jnp.minimum(most[i] // 8 + 1, TAPS // 8)
        accs = lax.fori_loop(0, free, functools.partial(group, False), zero)
        accs = lax.fori_loop(free, stop, functools.partial(group, True), accs)
        for p in range(parts):
            lanes = slice(p * HD, (p + 1) * HD)
            query = gate[pl.ds(base, tile), lanes].astype(F32)
            out[pl.ds(base, tile), lanes] = (query * accs[p]).astype(BF)
        return carry

    lax.fori_loop(0, rows // tile, row_tile, 0)


def filtered(extended, taps, reach, gate):
    rows, width = gate.shape
    tile = 64
    grouped = reach.reshape(rows // tile, tile)
    return pl.pallas_call(
        functools.partial(filter_kernel, tile),
        out_shape=jax.ShapeDtypeStruct((rows, width), BF),
        in_specs=[SMEM] * 2 + [VMEM] * 4,
        out_specs=VMEM,
        scratch_shapes=[pltpu.VMEM((8, rows + TAPS, width), F32)],
        compiler_params=pltpu.CompilerParams(vmem_limit_bytes=LIMIT),
        cost_estimate=pl.CostEstimate(
            flops=6 * TAPS * rows * width * 40, bytes_accessed=8 * rows * width, transcendentals=0
        ),
        name="filtered",
    )(jnp.min(grouped, axis=1), jnp.max(grouped, axis=1), extended, taps, reach, gate)


def attend_kernel(plan, first, last, me_ref, q_ref, begin_ref, *refs):
    refs = list(refs)
    pieces = [refs.pop(0) for _ in plan]
    before = [] if first else [refs.pop(0) for _ in range(3)]
    out = refs.pop(0) if last else None
    peak, total, running = refs
    me = me_ref[0]
    rows, width = q_ref.shape
    heads = width // HD
    chunk = 512
    scale = HD**-0.5 * math.log2(math.e)
    x = me % 4
    line = me // 4
    if first:
        peak[...] = jnp.full(peak.shape, NEG, F32)
        total[...] = jnp.zeros(total.shape, F32)
        running[...] = jnp.zeros(running.shape, F32)
    else:
        for now, then in zip((peak, total, running), before):
            now[...] = then[...]
    for piece, (dline, dx) in zip(pieces, plan):
        owner = (line - dline) * 4 + (x + dx) % 4

        @pl.when((line > 0) if dline else (owner <= me))
        def _(piece=piece, dline=dline, owner=owner):
            for base in range(0, rows, chunk):
                span = slice(base, base + chunk)
                begin = begin_ref[:, span]
                if dline:
                    open_row = begin <= owner * rows
                else:
                    key_at = owner * rows + lax.broadcasted_iota(jnp.int32, (rows, chunk), 0)
                    row_at = me * rows + base + lax.broadcasted_iota(jnp.int32, (1, chunk), 1)
                    allowed = (key_at <= row_at) & (key_at >= begin)
                for h in range(heads):
                    lanes = slice(h * HD, (h + 1) * HD)
                    keys = piece[:, lanes]
                    values = piece[:, width + h * HD : width + (h + 1) * HD]
                    scores = lax.dot_general(
                        keys, q_ref[span, lanes], (((1,), (1,)), ((), ())), preferred_element_type=F32
                    )
                    old = peak[h, :, span]
                    if dline:
                        top = jnp.max(scores, axis=0, keepdims=True)
                        new = jnp.where(open_row, jnp.maximum(old, top), old)
                        level = jnp.where(open_row, new, -NEG)
                    else:
                        scores = jnp.where(allowed, scores, NEG)
                        new = jnp.maximum(old, jnp.max(scores, axis=0, keepdims=True))
                        level = new
                    weights = jnp.exp2((scores - level) * scale)
                    factor = jnp.exp2((old - new) * scale)
                    peak[h, :, span] = new
                    total[h, :, span] = total[h, :, span] * factor + jnp.sum(weights, axis=0, keepdims=True)
                    update = lax.dot_general(
                        values, weights.astype(BF), (((0,), (0,)), ((), ())), preferred_element_type=F32
                    )
                    running[h, :, span] = running[h, :, span] * factor + update

    if last:
        for h in range(heads):
            out[:, h * HD : (h + 1) * HD] = (running[h] / total[h]).T.astype(BF)


def attend(me, queries, begins, plan, pieces, before=None, last=False):
    rows, width = queries.shape
    heads = width // HD
    state = [(heads, 1, rows), (heads, 1, rows), (heads, HD, rows)]
    if last:
        out_shape = jax.ShapeDtypeStruct((rows, width), BF)
        scratch = [pltpu.VMEM(s, F32) for s in state]
        out_specs = VMEM
    else:
        out_shape = tuple(jax.ShapeDtypeStruct(s, F32) for s in state)
        scratch = []
        out_specs = (VMEM,) * 3
    first = before is None
    before = () if first else tuple(before)
    return pl.pallas_call(
        functools.partial(attend_kernel, plan, first, last),
        out_shape=out_shape,
        in_specs=[SMEM] + [VMEM] * (2 + len(pieces) + len(before)),
        out_specs=out_specs,
        scratch_shapes=scratch,
        compiler_params=pltpu.CompilerParams(vmem_limit_bytes=LIMIT),
        cost_estimate=pl.CostEstimate(
            flops=4 * rows * rows * width * len(pieces) * 4,
            bytes_accessed=4 * (1 + len(pieces)) * rows * width,
            transcendentals=rows * rows * heads * len(pieces),
        ),
        name="attend",
    )(me, queries, begins, *pieces, *before)


def row_route(lines, pairs):
    return [(y * 4 + a, y * 4 + b) for y in lines for a, b in pairs]


ALL_UP = [(x, (x + 1) % 4) for x in range(4)]
ALL_DOWN = [(x, (x + 3) % 4) for x in range(4)]
ACROSS = [(x, 4 + x) for x in range(4)]


def attention(me, queries, begins, own):
    up = row_route((0,), ALL_UP) + row_route((1,), [(0, 1), (1, 2), (2, 3)])
    down = row_route((0,), ALL_DOWN) + row_route((1,), [(0, 3), (1, 0)])
    two_up = row_route((0,), [(x, (x + 2) % 4) for x in range(4)]) + row_route((1,), [(0, 2), (1, 3)])
    below = send(own, ACROSS, "seq")
    left = send(own, up, "seq")
    right = send(own, down, "seq")
    opposite = send(own, two_up, "seq")
    run = functools.partial(attend, me, queries, begins)
    state = run(((0, 0),), [own])
    below, state = lax.optimization_barrier((below, state))
    far_left = send(below, row_route((1,), ALL_UP), "seq")
    far_right = send(below, row_route((1,), ALL_DOWN), "seq")
    state = run(((0, 3), (0, 1)), [left, right], state)
    opposite, state = lax.optimization_barrier((opposite, state))
    far_opposite = send(opposite, ACROSS, "seq")
    state = run(((0, 2), (1, 0)), [opposite, below], state)
    far_left, far_right, state = lax.optimization_barrier((far_left, far_right, state))
    state = run(((1, 3), (1, 1)), [far_left, far_right], state)
    far_opposite, state = lax.optimization_barrier((far_opposite, state))
    return run(((1, 2),), [far_opposite], state, True)


def segment_begin(positions, seg_starts):
    below = seg_starts[None, :] <= positions[:, None]
    return jnp.max(jnp.where(below, seg_starts[None, :], 0), axis=1)


def rotation_tables(positions):
    half_dim = HD // 2
    freqs = 10000.0 ** (-2.0 * jnp.arange(half_dim, dtype=F32) / HD)
    angles = positions.astype(F32)[:, None] * freqs[None, :]
    cosine = jnp.cos(angles)
    sine = jnp.sin(angles)
    return jnp.concatenate([cosine, cosine], axis=1), jnp.concatenate([-sine, sine], axis=1)


def shards(
    tokens,
    seg_starts,
    gain_hyena,
    w_hyena_in,
    hyena_filter,
    w_hyena_out,
    gain_attn,
    w_attn_in,
    w_attn_out,
):
    rows, width = tokens.shape
    me = lax.axis_index("seq").astype(jnp.int32)
    order = relative_order(lax.axis_index("tensor"))
    positions = me * rows + jnp.arange(rows, dtype=jnp.int32)
    begins = segment_begin(positions, seg_starts)
    reach = jnp.where(begins == 0, TAPS, positions - begins)[:, None]
    begins = begins[None, :]
    tables = rotation_tables(positions)

    def summed_over_tensor(values, weight):
        other = spread(values, weight, order[8:])
        return scatter_tensor(spread(values, weight, order[:8]), other)

    def stacked(weight):
        return weight.transpose(1, 0, 2)

    gain_hyena = gain_hyena.reshape(16, 1, width)
    gain_attn = gain_attn.reshape(16, 1, width)
    blocks = gather_tensor(tokens_with_squares(tokens))
    product, gate = project((1, 2, 0), "hyena", blocks, order, gain_hyena, stacked(w_hyena_in))
    rim = send(product[rows - TAPS :], [(i, i + 1) for i in range(7)], "seq")
    tail = filtered(product, hyena_filter, reach[TAPS:], gate[TAPS:])
    head = filtered(
        jnp.concatenate([rim, product[:TAPS]], axis=0), hyena_filter, reach[:TAPS], gate[:TAPS]
    )
    gated = jnp.concatenate([head, tail], axis=0)
    middle = tokens.astype(F32) + summed_over_tensor(gated, w_hyena_out)
    blocks = gather_tensor(with_squares(middle))
    (own,) = project((1, 2), "attn", blocks, order, gain_attn, stacked(w_attn_in), tables)
    (queries,) = project((0,), "attn", blocks, order, gain_attn, stacked(w_attn_in), tables)
    context = attention(me[None], queries, begins, own)
    return middle + summed_over_tensor(context, w_attn_out)


def solution(mesh):
    placed = (
        P("seq", "tensor"),
        P(),
        P(),
        P(None, None, "tensor"),
        P(None, "tensor"),
        P("tensor", None),
        P(),
        P(None, None, "tensor"),
        P("tensor", None),
    )
    return jax.shard_map(
        shards, mesh=mesh, in_specs=placed, out_specs=P("seq", "tensor"), check_vma=False
    )
```
